32 devices in a mesh: samp: 8 (over z, core), feat: 4 (over y, x).
Axes of the slice: x: 2, y: 2, z: 4, core: 2. Of those that a mesh axis runs over, the one named last changes fastest.
Arguments:
- differences: bfloat16 [4608, 131072], P('samp', 'feat'), may hold values from -600 to 600
- start_block: bfloat16 [64, 131072], P(None, 'feat'), may hold values from -6 to 6
Outputs:
- directions: float32 [64, 131072], P(None, 'feat')
- layer_scores: float32 [16, 64], P('feat')
The draws below stay inside these ranges and needn't reach their ends.
All inputs are finite; a program needn't handle non-finite values.
Results may differ from the reference program's by a relative error of at most 0.0043.
Values may be sent and summed in bfloat16 or wider, within the bound.
No kernel may reach another device: no remote copies, remote signals or barrier semaphores. Data moves between devices by JAX's collectives and lax.ppermute only.
A program may use at most 192 MiB of HBM per device.

```python
import math
import jax
import jax.numpy as jnp
from jax import lax

WIDTH = 8192
LAYERS = 16
K = 64
ITERS = 2
NS = 4608
FEATURES = 131072


def draw_differences(key, part):
    keys = jax.random.split(key, 3)
    row_pos = jnp.arange(NS, dtype=jnp.float32) / NS
    col_pos = jnp.arange(FEATURES, dtype=jnp.float32) / FEATURES
    row_scale = (1.0 + 2.0 * row_pos) * jnp.exp(jax.random.uniform(keys[0], (NS,), jnp.float32) * jnp.log(10.0))
    col_scale = (1.0 + 2.0 * col_pos) * jnp.exp(jax.random.uniform(keys[1], (FEATURES,), jnp.float32) * jnp.log(10.0))
    noise = jnp.clip(jax.random.normal(keys[2], (NS, FEATURES), jnp.float32), -6.0, 6.0)
    values = 0.1 * noise * row_scale[:, None] * col_scale[None, :]
    return jnp.clip(values, -600.0, 600.0).astype(jnp.bfloat16)


def level_of(stream_key, dims, cuts, low, high):
    gain = 1.0
    for position, parts in cuts:
        draws = jax.random.uniform(jax.random.fold_in(jax.random.fold_in(stream_key, 6), position), (parts,), jnp.float32, low / len(cuts), high / len(cuts))
        gain = gain * jnp.repeat(jnp.exp(draws), dims[position] // parts).reshape((-1,) + (1,) * (len(dims) - 1 - position))
    return gain


def normal_values(stream_key, extent, spread, reach, pieces=(), kind=jnp.bfloat16):
    factor_of = level_of(stream_key, extent, pieces, -0.22, 0.18) if pieces else 1.0
    array = jax.random.normal(stream_key, extent, jnp.float32) * spread * factor_of
    return jnp.minimum(jnp.maximum(array, -reach), reach).astype(kind)


def setup_inputs(seed: int = 0) -> dict:
    splits = jax.random.split(jax.random.key(seed), 3)
    differences = draw_differences(jax.random.fold_in(splits[2], 71), 0)
    start_block = normal_values(splits[1], (K, FEATURES), 1.0, 6.0, ((1, 4),))
    return dict(differences=differences, start_block=start_block)


def reference(differences, start_block):
    block = start_block
    basis = None
    for step in range(ITERS):
        projected = jnp.dot(block.astype(jnp.float32), differences.T.astype(jnp.float32), preferred_element_type=jnp.float32).astype(jnp.bfloat16)
        pulled = jnp.dot(projected.astype(jnp.float32), differences.astype(jnp.float32), preferred_element_type=jnp.float32)
        gram = jnp.dot(pulled, pulled.T, precision=lax.Precision.HIGHEST)
        lower = jnp.linalg.cholesky(gram)
        basis = lax.linalg.triangular_solve(lower, pulled, left_side=True, lower=True)
        block = basis.astype(jnp.bfloat16)
    directions = basis * math.sqrt(FEATURES)
    score_rows = []
    for layer in range(LAYERS):
        piece = differences[:, layer * WIDTH:(layer + 1) * WIDTH]
        part = block[:, layer * WIDTH:(layer + 1) * WIDTH]
        along = jnp.dot(part.astype(jnp.float32), piece.T.astype(jnp.float32), preferred_element_type=jnp.float32)
        captured = lax.optimization_barrier(jnp.sum(along * along, axis=1))
        wide = piece.astype(jnp.float32)
        energy = jnp.sum(wide * wide)
        score_rows.append(FEATURES * captured / (energy + 1e-06))
    return (directions, jnp.stack(score_rows, axis=0))
```

```python
import functools
import math

import jax
import jax.numpy as jnp
from jax import lax
from jax.experimental import pallas as pl
from jax.experimental.pallas import tpu as pltpu
from jax.sharding import PartitionSpec as P

WIDTH = 8192
ITERS = 2
F32 = jnp.float32
BF16 = jnp.bfloat16
HIGHEST = lax.Precision.HIGHEST
VMEM_LIMIT = 48 * 1024 * 1024

TILE = 2048
CHUNK = 2048
PIECES = 4

VMEM = pl.BlockSpec(memory_space=pltpu.VMEM)
SMEM = pl.BlockSpec(memory_space=pltpu.SMEM)
ANY = pl.BlockSpec(memory_space=pl.ANY)


def dot_nt(a, b):
    return lax.dot_general(a, b, (((1,), (1,)), ((), ())), preferred_element_type=F32)


def dot_nn(a, b, precision=None):
    return lax.dot_general(
        a, b, (((1,), (0,)), ((), ())), precision=precision, preferred_element_type=F32
    )


def first_pass_kernel(sends, per_piece, per_layer, base_ref, block_ref, diff_ref, *outs):
    del base_ref
    step = pl.program_id(0)
    proj_ref, energy_ref = outs[0], outs[1]

    @pl.when(step == 0)
    def _():
        proj_ref[...] = jnp.zeros_like(proj_ref)

    @pl.when(step % per_layer == 0)
    def _():
        energy_ref[...] = jnp.zeros_like(energy_ref)

    proj_ref[...] += dot_nt(block_ref[...], diff_ref[...])

    def squares(i, acc):
        rows = diff_ref[pl.ds(pl.multiple_of(i * 16, 16), 16), :].astype(F32)
        return acc + rows[:8] * rows[:8] + rows[8:] * rows[8:]

    acc = lax.fori_loop(
        0, diff_ref.shape[0] // 16, squares, jnp.zeros((8, diff_ref.shape[1]), F32), unroll=4
    )
    folded = acc[:, :128]
    for j in range(1, diff_ref.shape[1] // 128):
        folded = folded + acc[:, j * 128 : (j + 1) * 128]
    energy_ref[...] += folded

    for piece in range(sends):

        @pl.when(step // per_piece == piece)
        def _(piece=piece):
            outs[2 + piece][...] = diff_ref[...]


def first_pass(block, differences, which_half, send):
    rows, cols = differences.shape
    k = block.shape[0]
    half = cols // 2
    steps = half // TILE
    per_layer = WIDTH // TILE
    layers_half = half // WIDTH
    per_piece = steps // PIECES
    sends = PIECES if send else 0

    def piece_map(piece, i, base):
        return (0, jnp.clip(i - piece * per_piece, 0, per_piece - 1))

    out_shape = [
        jax.ShapeDtypeStruct((k, rows), F32),
        jax.ShapeDtypeStruct((layers_half * 8, 128), F32),
    ] + [jax.ShapeDtypeStruct((rows, half // PIECES), BF16) for _ in range(sends)]
    out_specs = [
        pl.BlockSpec((k, rows), lambda i, base: (0, 0)),
        pl.BlockSpec((8, 128), lambda i, base: (i // per_layer, 0)),
    ] + [pl.BlockSpec((rows, TILE), functools.partial(piece_map, piece)) for piece in range(sends)]
    return pl.pallas_call(
        functools.partial(first_pass_kernel, sends, per_piece, per_layer),
        out_shape=out_shape,
        grid_spec=pltpu.PrefetchScalarGridSpec(
            num_scalar_prefetch=1,
            grid=(steps,),
            in_specs=[
                pl.BlockSpec((k, TILE), lambda i, base: (0, base[0] * steps + i)),
                pl.BlockSpec((rows, TILE), lambda i, base: (0, base[0] * steps + i)),
            ],
            out_specs=out_specs,
        ),
        cost_estimate=pl.CostEstimate(
            flops=2 * k * rows * half, bytes_accessed=rows * half * 4, transcendentals=0
        ),
        compiler_params=pltpu.CompilerParams(vmem_limit_bytes=VMEM_LIMIT),
        name="first_pass_send" if send else "first_pass",
    )(which_half.reshape(1).astype(jnp.int32), block, differences)


def step_kernel(ins, outs, at, back, *refs):
    names = list(ins) + list(outs) + ["pull_buf", "quad_buf", "sems"]
    r = dict(zip(names, refs))
    mid = r["meta"][0] > 0
    core = r["meta"][1]
    diff = r.get("diff")
    copies = []

    def fetch(buf, chunk, piece, sem):
        rows = diff.shape[0]
        half = diff.shape[1] // 2
        start = pl.multiple_of(core * half + chunk * CHUNK, CHUNK)
        own = pltpu.make_async_copy(
            diff.at[:, pl.ds(start, CHUNK)], buf.at[pl.ds(0, rows), :], r["sems"].at[sem]
        )
        inside = (chunk * CHUNK) % piece.shape[1]
        other = pltpu.make_async_copy(
            piece.at[:, pl.ds(inside, CHUNK)], buf.at[pl.ds(rows, rows), :], r["sems"].at[sem + 1]
        )
        own.start()
        other.start()
        return own, other

    if "pull_piece" in r:
        copies.append(fetch(r["pull_buf"], at, r["pull_piece"], 0))
    if "quad_piece" in r:
        copies.append(fetch(r["quad_buf"], back, r["quad_piece"], 2))

    if "pair" in r:
        r["pair"][...] = (r["own2"][...] + r["got_x"][...].astype(F32)).astype(BF16)
    total = None
    if "pair2" in r:
        total = (r["pair2"][...].astype(F32) + r["got_y"][...].astype(F32)).astype(BF16)
    if "pull_piece" in r:
        for copy in copies[0]:
            copy.wait()
        part = dot_nn(r["proj"][...], r["pull_buf"][...])
        r["own"][...] = part
        sent = part.astype(BF16)
        r["send_x"][...] = sent if total is None else jnp.where(mid, total, sent)
    elif total is not None:
        r["send_x"][...] = total
    if "quad_piece" in r:
        done = jnp.where(mid, r["sent_x2"][...], r["got_x"][...])
        for copy in copies[-1]:
            copy.wait()
        quad = dot_nt(done, r["quad_buf"][...])
        gram = dot_nt(done, done)
        r["quad"][...] = quad + r["quad_in"][...] if "quad_in" in r else quad
        r["gram"][...] = gram + r["gram_in"][...] if "gram_in" in r else gram
        if "total" in r:
            r["total"][...] = done


def pulled_steps(meta, proj, differences, pieces, perms, groups, keep):
    rows, cols = differences.shape
    k = proj.shape[0]
    half = cols // 2
    n = half // CHUNK
    swap, inner = perms
    per_piece = n // PIECES
    per_group = n // groups
    own, sent, pair, got_x, got_y, totals = {}, {}, {}, {}, {}, {}
    quads, quad, gram = [], None, None
    for t in range(n + 6):
        ins = {"meta": (meta, SMEM)}
        outs = {}
        if t < n:
            ins["proj"] = (proj, VMEM)
            ins["diff"] = (differences, ANY)
            ins["pull_piece"] = (pieces[t // per_piece], ANY)
            outs["own"] = ((k, CHUNK), F32)
        if 2 <= t < n + 2:
            ins["own2"] = (own[t - 2], VMEM)
            ins["got_x"] = (got_x[t - 2], VMEM)
            outs["pair"] = ((k, CHUNK), BF16)
        if 4 <= t < n + 4:
            ins["pair2"] = (pair[t - 2], VMEM)
            ins["got_y"] = (got_y[t - 2], VMEM)
        if t < n + 4:
            outs["send_x"] = ((k, CHUNK), BF16)
        back = t - 6
        if back >= 0:
            ins["got_x"] = (got_x[t - 2], VMEM)
            ins["sent_x2"] = (sent[t - 2], VMEM)
            ins["diff"] = (differences, ANY)
            ins["quad_piece"] = (pieces[back // per_piece], ANY)
            if back % per_group:
                ins["quad_in"] = (quad, VMEM)
            if back:
                ins["gram_in"] = (gram, VMEM)
            outs["quad"] = ((k, 2 * rows), F32)
            outs["gram"] = ((k, k), F32)
            if keep:
                outs["total"] = ((k, CHUNK), BF16)
        work = (t < n) + (back >= 0)
        result = pl.pallas_call(
            functools.partial(step_kernel, tuple(ins), tuple(outs), t, back),
            out_shape=[jax.ShapeDtypeStruct(*outs[name]) for name in outs],
            in_specs=[spec for _, spec in ins.values()],
            out_specs=[VMEM] * len(outs),
            scratch_shapes=[
                pltpu.VMEM((2 * rows, CHUNK), BF16),
                pltpu.VMEM((2 * rows, CHUNK), BF16),
                pltpu.SemaphoreType.DMA((4,)),
            ],
            cost_estimate=pl.CostEstimate(
                flops=work * 4 * k * rows * CHUNK,
                bytes_accessed=work * 4 * rows * CHUNK + 8 * k * CHUNK,
                transcendentals=0,
            ),
            compiler_params=pltpu.CompilerParams(vmem_limit_bytes=VMEM_LIMIT),
            name=f"pulled_step_{t}",
        )(*[value for value, _ in ins.values()])
        r = dict(zip(outs, result))
        if t < n:
            own[t] = r["own"]
        if 2 <= t < n + 2:
            pair[t] = r["pair"]
            got_y[t] = lax.ppermute(pair[t], "samp", inner)
        if t < n + 4:
            sent[t] = r["send_x"]
            got_x[t] = lax.ppermute(sent[t], "samp", swap)
        if back >= 0:
            quad, gram = r["quad"], r["gram"]
            if (back + 1) % per_group == 0:
                quads.append(quad)
            if keep:
                totals[back] = r["total"]
    return quads, gram, [totals[c] for c in sorted(totals)]


def inverse_factor(gram):
    k = gram.shape[0]
    lane = lax.broadcasted_iota(jnp.int32, (8, 2 * k), 1)
    sub = lax.broadcasted_iota(jnp.int32, (8, 2 * k), 0)
    blocks = []
    for b in range(k // 8):
        left = jnp.concatenate([gram[b * 8 : (b + 1) * 8, :], jnp.zeros((8, k), F32)], axis=1)
        blocks.append(jnp.where(lane == sub + (k + b * 8), 1.0, left))
    scale = [jnp.zeros((8, 1), F32) for _ in blocks]
    sub1 = lax.broadcasted_iota(jnp.int32, (8, 1), 0)
    for j in range(k):
        b, i = divmod(j, 8)
        row = blocks[b][i : i + 1, :]
        pivot = row[:, j : j + 1]
        scale[b] = jnp.where(sub1 == i, pivot, scale[b])
        scaled = row / pivot
        for c in range(b, k // 8):
            factor = blocks[c][:, j : j + 1]
            if c == b:
                factor = jnp.where(sub1 > i, factor, 0.0)
            blocks[c] = blocks[c] - factor * scaled
    return jnp.concatenate(
        [block[:, k:] * (1.0 / jnp.sqrt(s)) for block, s in zip(blocks, scale)], axis=0
    )


def project_kernel(gram_ref, quad_ref, proj_ref):
    inverse = inverse_factor(gram_ref[...])
    proj_ref[...] = dot_nn(inverse, quad_ref[...], HIGHEST).astype(BF16)


def next_projection(gram, quad):
    return pl.pallas_call(
        project_kernel,
        out_shape=jax.ShapeDtypeStruct(quad.shape, BF16),
        in_specs=[VMEM, VMEM],
        out_specs=VMEM,
        compiler_params=pltpu.CompilerParams(vmem_limit_bytes=VMEM_LIMIT),
        name="next_projection",
    )(gram, quad)


def score_kernel(groups, gram_ref, *refs):
    quads, energy_ref, inverse_ref, out_ref = refs[:groups], *refs[groups:]
    inverse = inverse_factor(gram_ref[...])
    inverse_ref[...] = inverse
    out = energy_ref[...]
    lane = lax.broadcasted_iota(jnp.int32, out.shape, 1)
    for g in range(groups):
        along = dot_nn(inverse, quads[g][...], HIGHEST)
        out = jnp.where(lane == g, jnp.sum(along * along, axis=1, keepdims=True), out)
    out_ref[...] = out


def score_parts(gram, quads, energy):
    k = gram.shape[0]
    return pl.pallas_call(
        functools.partial(score_kernel, len(quads)),
        out_shape=[jax.ShapeDtypeStruct((k, k), F32), jax.ShapeDtypeStruct((k, 128), F32)],
        in_specs=[VMEM] * (2 + len(quads)),
        out_specs=[VMEM, VMEM],
        compiler_params=pltpu.CompilerParams(vmem_limit_bytes=VMEM_LIMIT),
        name="score_parts",
    )(gram, *quads, energy)


def directions_kernel(count, scale, meta_ref, inverse_ref, *refs):
    totals, out_ref, in_buf, out_buf, in_sems, out_sems = refs[: 2 * count], *refs[2 * count :]
    core = meta_ref[1]
    width = totals[0].shape[1]
    loads = [
        pltpu.make_async_copy(totals[i], in_buf.at[i], in_sems.at[i]) for i in range(2 * count)
    ]
    for load in loads:
        load.start()
    inverse = inverse_ref[...] * scale
    high = inverse.astype(BF16)
    low = (inverse - high.astype(F32)).astype(BF16)
    stores = []
    for i in range(2 * count):
        loads[i].wait()
        piece = in_buf[i]
        out_buf[i] = dot_nn(high, piece) + dot_nn(low, piece)
        side = core if i < count else 1 - core
        start = pl.multiple_of((side * count + i % count) * width, width)
        store = pltpu.make_async_copy(
            out_buf.at[i], out_ref.at[:, pl.ds(start, width)], out_sems.at[i]
        )
        store.start()
        stores.append(store)
    for store in stores:
        store.wait()


def make_directions(meta, inverse, own, other, scale):
    count = len(own)
    k, width = own[0].shape
    return pl.pallas_call(
        functools.partial(directions_kernel, count, scale),
        out_shape=jax.ShapeDtypeStruct((k, 2 * count * width), F32),
        in_specs=[SMEM, VMEM] + [ANY] * (2 * count),
        out_specs=ANY,
        scratch_shapes=[
            pltpu.VMEM((2 * count, k, width), BF16),
            pltpu.VMEM((2 * count, k, width), F32),
            pltpu.SemaphoreType.DMA((2 * count,)),
            pltpu.SemaphoreType.DMA((2 * count,)),
        ],
        cost_estimate=pl.CostEstimate(
            flops=8 * k * k * count * width,
            bytes_accessed=12 * k * count * width,
            transcendentals=0,
        ),
        compiler_params=pltpu.CompilerParams(vmem_limit_bytes=VMEM_LIMIT),
        name="directions",
    )(meta, inverse, *own, *other)


def pipelined(samp, feat, differences, start_block):
    rows, cols = differences.shape
    layers_half = cols // WIDTH // 2
    features = cols * feat
    me = lax.axis_index("samp")
    core = me % 2
    chip = me // 2
    mid = (chip == 1) | (chip == 2)
    meta = jnp.stack([mid.astype(jnp.int32), core.astype(jnp.int32)])

    cores = [(d, d ^ 1) for d in range(samp)]
    swap = [(d, d ^ 2) for d in range(samp)]
    inner = [(d, d ^ 6) for d in range(samp) if d // 2 in (1, 2)]
    bits = [1 << b for b in range(feat.bit_length() - 1)]

    def other_core(x):
        return lax.ppermute(x, "samp", cores)

    def over_feat(x):
        split = x.shape[0] // 2
        parts = [x[:split], x[split:]]
        orders = [bits, bits[::-1]]
        for hop in range(len(bits)):
            parts = [
                part + lax.ppermute(part, "feat", [(d, d ^ order[hop]) for d in range(feat)])
                for part, order in zip(parts, orders)
            ]
        return jnp.concatenate(parts, axis=0)

    sent = first_pass(start_block, differences, 1 - core, True)
    pieces = [other_core(piece) for piece in sent[2:]]
    kept = first_pass(start_block, differences, core, False)
    mine = over_feat(sent[0] + kept[0]).astype(BF16)

    energy_sent = jnp.sum(sent[1].reshape(layers_half, -1), axis=1)
    energy_kept = jnp.sum(kept[1].reshape(layers_half, -1), axis=1)
    energies = jnp.concatenate([energy_kept, energy_sent])
    energy_tile = jnp.zeros((start_block.shape[0], 128), F32)
    energy_tile = energy_tile.at[:, layers_half : 3 * layers_half].set(energies[None, :])

    for step in range(ITERS):
        last = step == ITERS - 1
        proj = jnp.concatenate([mine, other_core(mine)], axis=1)
        quads, gram, totals = pulled_steps(
            meta, proj, differences, pieces, (swap, inner), layers_half if last else 1, last
        )
        if not last:
            quad = quads[0]
            both = jnp.concatenate([quad[:, :rows], gram], axis=1)
            theirs = jnp.concatenate([quad[:, rows:], gram], axis=1)
            both = over_feat(both + other_core(theirs))
            mine = next_projection(both[:, rows:], both[:, :rows])

    per = len(totals) // PIECES
    own = [jnp.concatenate(totals[i * per : (i + 1) * per], axis=1) for i in range(PIECES)]
    other = [other_core(total) for total in own]
    gram = gram + other_core(gram)
    gram = over_feat(gram)
    inverse, scores = score_parts(gram, quads, energy_tile)
    near, far, cross = (
        lax.ppermute(scores, "samp", [(d, d ^ bit) for d in range(samp)]) for bit in (2, 4, 6)
    )
    scores = (scores + near) + (far + cross)
    theirs = other_core(scores)
    directions = make_directions(meta, inverse, own, other, math.sqrt(features))
    lh = layers_half
    own_energy = scores[:1, lh : 2 * lh] + theirs[:1, 2 * lh : 3 * lh]
    other_energy = scores[:1, 2 * lh : 3 * lh] + theirs[:1, lh : 2 * lh]
    own_scores = features * scores[:, :lh] / (own_energy + 1e-06)
    other_scores = features * theirs[:, :lh] / (other_energy + 1e-06)
    first = jnp.where(core == 0, own_scores, other_scores)
    second = jnp.where(core == 0, other_scores, own_scores)
    return (directions, jnp.concatenate([first, second], axis=1).T)


def orthonormal(pulled, gram):
    lower = jnp.linalg.cholesky(gram)
    return lax.linalg.triangular_solve(lower, pulled, left_side=True, lower=True)


def plain(samp, feat, differences, start_block):
    features = differences.shape[1] * feat
    block = start_block
    basis = None
    for step in range(ITERS):
        partial_rows = dot_nt(block, differences)
        projected = lax.psum(partial_rows, "feat").astype(BF16)
        partial_cols = jnp.dot(projected, differences, preferred_element_type=F32)
        pulled = lax.psum(partial_cols, "samp")
        local_gram = jnp.dot(pulled, pulled.T, precision=HIGHEST)
        gram = lax.psum(local_gram, "feat")
        basis = orthonormal(pulled, gram)
        block = basis.astype(BF16)
    directions = basis * math.sqrt(features)
    samples = differences.shape[0]
    layers_here = differences.shape[1] // WIDTH
    stacked = differences.reshape(samples, layers_here, WIDTH)
    block_layers = block.reshape(block.shape[0], layers_here, WIDTH)
    along = jnp.einsum("kjw,sjw->jks", block_layers, stacked, preferred_element_type=F32)
    captured = jnp.sum(along * along, axis=2)
    energy = jnp.einsum("sjw,sjw->j", stacked, stacked, preferred_element_type=F32)
    captured, energy = lax.psum((captured, energy), "samp")
    layer_scores = features * captured / (energy[:, None] + 1e-06)
    return (directions, layer_scores)


def solution(mesh):
    samp, feat = mesh.shape["samp"], mesh.shape["feat"]

    def on_device(differences, start_block):
        even = differences.shape[1] % (2 * WIDTH) == 0 and differences.shape[0] % 16 == 0
        paired = samp == 8 and feat & (feat - 1) == 0
        form = pipelined if even and paired else plain
        return form(samp, feat, differences, start_block)

    in_specs = (P("samp", "feat"), P(None, "feat"))
    out_specs = (P(None, "feat"), P("feat", None))
    return jax.shard_map(
        on_device, mesh=mesh, in_specs=in_specs, out_specs=out_specs, check_vma=False
    )
```

```python
import functools
import math

import jax
import jax.numpy as jnp
from jax import lax
from jax.experimental import pallas as pl
from jax.experimental.pallas import tpu as pltpu
from jax.sharding import PartitionSpec as P

WIDTH = 8192
ITERS = 2
F32 = jnp.float32
BF16 = jnp.bfloat16
HIGHEST = lax.Precision.HIGHEST
MIB = 1024 * 1024
PASS_LIMIT = 16 * MIB
STEP_LIMIT = 19 * MIB
SMALL_LIMIT = 4 * MIB
LAST_LIMIT = 20 * MIB

TILE = 1024
SLOTS = 6
PLAN = (1,) * 8
JOINS = 4
PIECES = (1, 1, 2)

VMEM = pl.BlockSpec(memory_space=pltpu.VMEM)
SMEM = pl.BlockSpec(memory_space=pltpu.SMEM)
ANY = pl.BlockSpec(memory_space=pl.ANY)
BLOCK = 512


def dot_nt(a, b):
    return lax.dot_general(a, b, (((1,), (1,)), ((), ())), preferred_element_type=F32)


def dot_nn(a, b, precision=None):
    return lax.dot_general(
        a, b, (((1,), (0,)), ((), ())), precision=precision, preferred_element_type=F32
    )


def spans(half, plan):
    unit = half // sum(plan)
    return [(sum(plan[:i]) * unit, size * unit) for i, size in enumerate(plan)]


def part_of(plan, half, column):
    return [first <= column < first + width for first, width in spans(half, plan)].index(True)


def first_pass_kernel(send, steps, per_layer, side_ref, block_ref, diff_ref, *refs):
    begun = None if send else refs[0]
    refs = refs if send else refs[1:]
    proj_ref, energy_ref = refs[0], refs[1]
    tiles, blocks, in_sems, block_sems, out_sems = refs[-5:]
    base = side_ref[0] * (steps * TILE)

    def columns(i):
        return pl.ds(pl.multiple_of(base + i * TILE, TILE), TILE)

    loads, stores = [], []
    for i in range(steps):
        at = i % SLOTS
        loads.append(
            (
                pltpu.make_async_copy(diff_ref.at[:, columns(i)], tiles.at[at], in_sems.at[at]),
                pltpu.make_async_copy(block_ref.at[:, columns(i)], blocks.at[at], block_sems.at[at]),
            )
        )
        if send:
            piece = part_of(PIECES, steps * TILE, i * TILE)
            inside = i * TILE - spans(steps * TILE, PIECES)[piece][0]
            place = refs[2 + piece].at[:, pl.ds(inside, TILE)]
            stores.append(pltpu.make_async_copy(tiles.at[at], place, out_sems.at[at]))
    ahead = SLOTS - 1
    for load in loads[:ahead]:
        load[0].start()
        load[1].start()
    proj = None
    for i in range(steps):
        at = i % SLOTS
        loads[i][0].wait()
        loads[i][1].wait()
        if send:
            stores[i].start()
        if i + ahead < steps:
            if send and i:
                stores[i - 1].wait()
            loads[i + ahead][0].start()
            loads[i + ahead][1].start()
        part = dot_nt(blocks[at], tiles[at])
        proj = part if proj is None else proj + part
        acc = jnp.zeros((8, TILE), F32)
        for r in range(0, tiles.shape[1], 16):
            rows = tiles[at, r : r + 16, :].astype(F32)
            acc = acc + rows[:8] * rows[:8] + rows[8:] * rows[8:]
        folded = acc[:, :128]
        for j in range(1, TILE // 128):
            folded = folded + acc[:, j * 128 : (j + 1) * 128]
        layer = pl.ds(i // per_layer * 8, 8)
        if i % per_layer:
            folded = folded + energy_ref[layer, :]
        energy_ref[layer, :] = folded
    proj_ref[...] = proj if begun is None else proj + begun[...]
    for store in stores[-SLOTS:]:
        store.wait()


def first_pass(block, differences, side, begun=None):
    send = begun is None
    rows, cols = differences.shape
    k = block.shape[0]
    half = cols // 2
    widths = [width for _, width in spans(half, PIECES)] if send else []
    return pl.pallas_call(
        functools.partial(first_pass_kernel, send, half // TILE, WIDTH // TILE),
        out_shape=[
            jax.ShapeDtypeStruct((k, rows), F32),
            jax.ShapeDtypeStruct((half // WIDTH * 8, 128), F32),
        ]
        + [jax.ShapeDtypeStruct((rows, width), BF16) for width in widths],
        in_specs=[SMEM, ANY, ANY] + [VMEM] * (not send),
        out_specs=[VMEM, VMEM] + [ANY] * len(widths),
        scratch_shapes=[
            pltpu.VMEM((SLOTS, rows, TILE), BF16),
            pltpu.VMEM((SLOTS, k, TILE), BF16),
            pltpu.SemaphoreType.DMA((SLOTS,)),
            pltpu.SemaphoreType.DMA((SLOTS,)),
            pltpu.SemaphoreType.DMA((SLOTS,)),
        ],
        cost_estimate=pl.CostEstimate(
            flops=2 * k * rows * half, bytes_accessed=rows * half * 4, transcendentals=0
        ),
        compiler_params=pltpu.CompilerParams(vmem_limit_bytes=PASS_LIMIT),
        name="first_pass_send" if send else "first_pass",
    )(side.reshape(1).astype(jnp.int32), block, differences, *([] if send else [begun]))


def fetch(core, diff, piece, chunk, out, sems):
    rows, cols = diff.shape
    first, width = chunk
    inside = first - spans(cols // 2, PIECES)[part_of(PIECES, cols // 2, first)][0]
    start = pl.multiple_of(core * (cols // 2) + first, BLOCK)
    mine = diff.at[:, pl.ds(start, width)]
    theirs = piece.at[:, pl.ds(inside, width)]
    return [
        pltpu.make_async_copy(mine, out.at[pl.ds(0, rows), :], sems.at[0]),
        pltpu.make_async_copy(theirs, out.at[pl.ds(rows, rows), :], sems.at[1]),
    ]


def step_kernel(ins, outs, pull_next, quad_next, *refs):
    r = dict(zip(list(ins) + list(outs) + ["pull_sems", "quad_sems"], refs))
    mid = r["meta"][0] > 0
    copies = []
    for name, chunk in (("pull", pull_next), ("quad", quad_next)):
        if chunk is not None:
            place = (r[name + "_piece"], chunk, r[name + "_out"], r[name + "_sems"])
            copies += fetch(r["meta"][1], r["diff"], *place)
    for copy in copies:
        copy.start()
    if "pair" in r:
        for c in range(0, r["pair"].shape[1], BLOCK):
            at = pl.ds(c, BLOCK)
            r["pair"][:, at] = (r["own2"][:, at] + r["got_x"][:, at].astype(F32)).astype(BF16)
    if "send_x" in r:
        pulled = r["own"].shape[1] if "own" in r else 0
        summed = r["pair2"].shape[1] if "pair2" in r else 0
        for c in range(0, max(pulled, summed), BLOCK):
            at = pl.ds(c, BLOCK)
            sent = None
            if c < pulled:
                sent = dot_nn(r["proj"][...], r["pull_in"][:, at])
                r["own"][:, at] = sent
            if c < summed:
                total = r["pair2"][:, at].astype(F32) + r["got_y"][:, at].astype(F32)
                sent = total if sent is None else jnp.where(mid, total, sent)
            r["send_x"][:, at] = sent.astype(BF16)
    if "quad_in" in r:
        width = r["quad_in"].shape[1]
        done = jnp.where(mid, r["sent_x2"][:, :width], r["got_x"][:, :width])
        if "total" in r:
            joined = r["total"].shape[1] - width
            if joined:
                r["total"][:, pl.ds(0, joined)] = r["total_in"][...]
            r["total"][:, pl.ds(joined, width)] = done
        quad = dot_nt(done, r["quad_in"][...])
        gram = dot_nt(done, done)
        r["quad"][...] = quad + r["quad_sum"][...] if "quad_sum" in r else quad
        r["gram"][...] = gram + r["gram_sum"][...] if "gram_sum" in r else gram
    for copy in copies:
        copy.wait()


def first_chunk_kernel(chunk, meta_ref, diff_ref, piece_ref, out_ref, sems):
    copies = fetch(meta_ref[1], diff_ref, piece_ref, chunk, out_ref, sems)
    for copy in copies:
        copy.start()
    for copy in copies:
        copy.wait()


def first_chunk(meta, differences, piece):
    rows, cols = differences.shape
    chunk = spans(cols // 2, PLAN)[0]
    return pl.pallas_call(
        functools.partial(first_chunk_kernel, chunk),
        out_shape=jax.ShapeDtypeStruct((2 * rows, chunk[1]), BF16),
        in_specs=[SMEM, ANY, ANY],
        out_specs=VMEM,
        scratch_shapes=[pltpu.SemaphoreType.DMA((2,))],
        compiler_params=pltpu.CompilerParams(vmem_limit_bytes=STEP_LIMIT),
        name="first_chunk",
    )(meta, differences, piece)


def pulled_steps(meta, proj, pull, differences, got, perms, layer, last):
    rows, cols = differences.shape
    k = proj.shape[0]
    half = cols // 2
    chunks = spans(half, PLAN)
    n = len(chunks)
    swap, inner = perms
    group = layer if last else half
    join = half // JOINS
    own, sent, pair, got_x, got_y = {}, {}, {}, {}, {}
    quads, quad, quad_buf, gram = [], None, None, None
    totals, total = [], None
    steps = n + 6
    for t in range(steps):
        ins = {"meta": (meta, SMEM)}
        outs = {}
        back = t - 6
        width = 0
        if t < n:
            width = chunks[t][1]
            ins["proj"] = (proj, VMEM)
            ins["pull_in"] = (pull, VMEM)
            outs["own"] = ((k, width), F32)
        if 2 <= t < n + 2:
            ins["own2"] = (own[t - 2], VMEM)
            ins["got_x"] = (got_x[t - 2], VMEM)
            outs["pair"] = ((k, chunks[t - 2][1]), BF16)
        if 4 <= t < n + 4:
            width = max(width, chunks[t - 4][1])
            ins["pair2"] = (pair[t - 2], VMEM)
            ins["got_y"] = (got_y[t - 2], VMEM)
        if t < n + 4:
            outs["send_x"] = ((k, width), BF16)
        if back >= 0:
            first, back_width = chunks[back]
            ins["got_x"] = (got_x[t - 2], VMEM)
            ins["sent_x2"] = (sent[t - 2], VMEM)
            ins["quad_in"] = (quad_buf, VMEM)
            if first % group:
                ins["quad_sum"] = (quad, VMEM)
            if back:
                ins["gram_sum"] = (gram, VMEM)
            outs["quad"] = ((k, 2 * rows), F32)
            outs["gram"] = ((k, k), F32)
            if last:
                if first % join:
                    ins["total_in"] = (total, VMEM)
                outs["total"] = ((k, first % join + back_width), BF16)
        pull_next, quad_next = None, None
        if t + 1 < n or (t == steps - 1 and not last):
            pull_next = chunks[t + 1 if t + 1 < n else 0]
            ins["diff"] = (differences, ANY)
            ins["pull_piece"] = (got[part_of(PIECES, half, pull_next[0])], ANY)
            outs["pull_out"] = ((2 * rows, pull_next[1]), BF16)
        if 0 <= back + 1 < n:
            quad_next = chunks[back + 1]
            ins["diff"] = (differences, ANY)
            ins["quad_piece"] = (got[part_of(PIECES, half, quad_next[0])], ANY)
            outs["quad_out"] = ((2 * rows, quad_next[1]), BF16)
        work = (chunks[t][1] if t < n else 0) + (chunks[back][1] if back >= 0 else 0)
        result = pl.pallas_call(
            functools.partial(step_kernel, tuple(ins), tuple(outs), pull_next, quad_next),
            out_shape=[jax.ShapeDtypeStruct(*outs[name]) for name in outs],
            in_specs=[spec for _, spec in ins.values()],
            out_specs=[VMEM] * len(outs),
            scratch_shapes=[
                pltpu.SemaphoreType.DMA((2,)),
                pltpu.SemaphoreType.DMA((2,)),
            ],
            cost_estimate=pl.CostEstimate(
                flops=4 * k * rows * work, bytes_accessed=4 * rows * work, transcendentals=0
            ),
            compiler_params=pltpu.CompilerParams(vmem_limit_bytes=STEP_LIMIT),
            name=f"pulled_step_{t}",
        )(*[value for value, _ in ins.values()])
        r = dict(zip(outs, result))
        pull, quad_buf = r.get("pull_out"), r.get("quad_out")
        if t < n:
            own[t] = r["own"]
        if 2 <= t < n + 2:
            pair[t] = r["pair"]
            got_y[t] = lax.ppermute(pair[t], "samp", inner)
        if t < n + 4:
            sent[t] = r["send_x"]
            got_x[t] = lax.ppermute(sent[t], "samp", swap)
        if back >= 0:
            quad, gram = r["quad"], r["gram"]
            if (first + back_width) % group == 0:
                quads.append(quad)
            total = r.get("total")
            if last and (first + back_width) % join == 0:
                totals.append(total)
    return quads, gram, totals, pull


def inverse_factor(gram):
    k = gram.shape[0]
    lane = lax.broadcasted_iota(jnp.int32, (8, 2 * k), 1)
    sub = lax.broadcasted_iota(jnp.int32, (8, 2 * k), 0)
    blocks = []
    for b in range(k // 8):
        left = jnp.concatenate([gram[b * 8 : (b + 1) * 8, :], jnp.zeros((8, k), F32)], axis=1)
        blocks.append(jnp.where(lane == sub + (k + b * 8), 1.0, left))
    scale = [jnp.zeros((8, 1), F32) for _ in blocks]
    sub1 = lax.broadcasted_iota(jnp.int32, (8, 1), 0)
    for j in range(k):
        b, i = divmod(j, 8)
        row = blocks[b][i : i + 1, :]
        pivot = row[:, j : j + 1]
        scale[b] = jnp.where(sub1 == i, pivot, scale[b])
        scaled = row / pivot
        for c in range(b, k // 8):
            factor = blocks[c][:, j : j + 1]
            if c == b:
                factor = jnp.where(sub1 > i, factor, 0.0)
            blocks[c] = blocks[c] - factor * scaled
    return jnp.concatenate(
        [block[:, k:] * (1.0 / jnp.sqrt(s)) for block, s in zip(blocks, scale)], axis=0
    )


def project_kernel(gram_ref, quad_ref, proj_ref):
    inverse = inverse_factor(gram_ref[...])
    proj_ref[...] = dot_nn(inverse, quad_ref[...], HIGHEST).astype(BF16)


def next_projection(gram, quad):
    return pl.pallas_call(
        project_kernel,
        out_shape=jax.ShapeDtypeStruct(quad.shape, BF16),
        in_specs=[VMEM, VMEM],
        out_specs=VMEM,
        compiler_params=pltpu.CompilerParams(vmem_limit_bytes=SMALL_LIMIT),
        name="next_projection",
    )(gram, quad)


def score_parts_kernel(groups, chips, gram_ref, kept_ref, sent_ref, *refs):
    quads, out_ref = refs[:groups], refs[groups]
    k = gram_ref.shape[0]
    row = lax.broadcasted_iota(jnp.int32, (k, k), 0)
    lane = lax.broadcasted_iota(jnp.int32, (k, k), 1)
    trace = jnp.sum(jnp.where(row == lane, gram_ref[...], 0.0), keepdims=True)
    scale = 1.0 / jnp.sqrt(trace)
    sub = lax.broadcasted_iota(jnp.int32, (8, k), 0)
    for g in range(groups):
        quad = quads[g][...] * scale
        at = pl.ds(g * k, k)
        out_ref[pl.ds(0, k), at] = lax.dot_general(
            quad,
            quad,
            (((1,), (1,)), ((), ())),
            precision=HIGHEST,
            preferred_element_type=F32,
        )
        kept = jnp.sum(kept_ref[pl.ds(g * 8, 8), :], keepdims=True)
        sent = jnp.sum(sent_ref[pl.ds(g * 8, 8), :], keepdims=True)
        rest = jnp.where(sub == 0, kept, jnp.where(sub == 1, sent, trace / chips))
        out_ref[pl.ds(k, 8), at] = rest


def score_parts(gram, quads, kept, sent, chips):
    k = gram.shape[0]
    return pl.pallas_call(
        functools.partial(score_parts_kernel, len(quads), chips),
        out_shape=jax.ShapeDtypeStruct((k + 8, len(quads) * k), F32),
        in_specs=[VMEM] * (3 + len(quads)),
        out_specs=VMEM,
        compiler_params=pltpu.CompilerParams(vmem_limit_bytes=SMALL_LIMIT),
        name="score_parts",
    )(gram, kept, sent, *quads)


def scores_kernel(groups, features, meta_ref, gram_ref, mine_ref, got_ref, inverse_ref, out_ref):
    k = gram_ref.shape[0]
    inverse = inverse_factor(gram_ref[...])
    inverse_ref[...] = inverse
    core = meta_ref[1]
    ones = jnp.ones((8, k), F32)
    mine, got = mine_ref[...], got_ref[...]
    low, high = jnp.where(core == 0, mine, got), jnp.where(core == 0, got, mine)
    for half, (one, two) in enumerate(((low, high), (high, low))):
        scaled = inverse * jnp.sqrt(one[k + 2 : k + 3, 0:1])
        for g in range(groups):
            at = slice(g * k, (g + 1) * k)
            moment = dot_nn(scaled, one[:k, at], HIGHEST) * scaled
            captured = lax.dot_general(
                ones,
                moment,
                (((1,), (1,)), ((), ())),
                precision=HIGHEST,
                preferred_element_type=F32,
            )[:1]
            energy = one[k : k + 1, at] + two[k + 1 : k + 2, at]
            out_ref[pl.ds(half * groups + g, 1), :] = features * captured / (energy + 1e-06)


def scores_of(meta, gram, mine, got, groups, features):
    k = gram.shape[0]
    return pl.pallas_call(
        functools.partial(scores_kernel, groups, features),
        out_shape=[
            jax.ShapeDtypeStruct((k, k), F32),
            jax.ShapeDtypeStruct((2 * groups, k), F32),
        ],
        in_specs=[SMEM, VMEM, VMEM, VMEM],
        out_specs=[VMEM, VMEM],
        compiler_params=pltpu.CompilerParams(vmem_limit_bytes=SMALL_LIMIT),
        name="scores",
    )(meta, gram, mine, got)


def directions_kernel(count, scale, meta_ref, inverse_ref, *refs):
    totals = refs[: 2 * count]
    out_ref, in_buf, out_buf, in_sems, out_sems = refs[2 * count :]
    core = meta_ref[1]
    width = totals[0].shape[1]
    loads = [
        pltpu.make_async_copy(totals[i], in_buf.at[i], in_sems.at[i]) for i in range(2 * count)
    ]
    for load in loads:
        load.start()
    inverse = inverse_ref[...] * scale
    high = inverse.astype(BF16)
    low = (inverse - high.astype(F32)).astype(BF16)
    stores = []
    for i in range(2 * count):
        loads[i].wait()
        for c in range(0, width, BLOCK):
            at = pl.ds(c, BLOCK)
            piece = in_buf[i, :, at]
            out_buf[i, :, at] = dot_nn(high, piece) + dot_nn(low, piece)
        side = core if i < count else 1 - core
        start = pl.multiple_of((side * count + i % count) * width, width)
        store = pltpu.make_async_copy(
            out_buf.at[i], out_ref.at[:, pl.ds(start, width)], out_sems.at[i]
        )
        store.start()
        stores.append(store)
    for store in stores:
        store.wait()


def make_directions(meta, inverse, totals, totals_far, scale):
    count = len(totals)
    k, width = totals[0].shape
    return pl.pallas_call(
        functools.partial(directions_kernel, count, scale),
        out_shape=jax.ShapeDtypeStruct((k, 2 * count * width), F32),
        in_specs=[SMEM, VMEM] + [ANY] * (2 * count),
        out_specs=ANY,
        scratch_shapes=[
            pltpu.VMEM((2 * count, k, width), BF16),
            pltpu.VMEM((2 * count, k, width), F32),
            pltpu.SemaphoreType.DMA((2 * count,)),
            pltpu.SemaphoreType.DMA((2 * count,)),
        ],
        cost_estimate=pl.CostEstimate(
            flops=8 * k * k * count * width,
            bytes_accessed=12 * k * count * width,
            transcendentals=0,
        ),
        compiler_params=pltpu.CompilerParams(vmem_limit_bytes=LAST_LIMIT),
        name="directions",
    )(meta, inverse, *totals, *totals_far)


def pipelined(samp, feat, differences, start_block):
    rows, cols = differences.shape
    layers_half = cols // WIDTH // 2
    features = cols * feat
    me = lax.axis_index("samp")
    core = me % 2
    chip = me // 2
    mid = (chip == 1) | (chip == 2)
    meta = jnp.stack([mid.astype(jnp.int32), core.astype(jnp.int32)])

    cores = [(d, d ^ 1) for d in range(samp)]
    swap = [(d, d ^ 2) for d in range(samp)]
    inner = [(d, d ^ 6 if d // 2 in (1, 2) else d ^ 1) for d in range(samp)]
    bits = [1 << b for b in range(feat.bit_length() - 1)]

    def other_core(x):
        return lax.ppermute(x, "samp", cores)

    def over_feat(x, beside=()):
        split = x.shape[0] // 2
        parts = [x[:split], x[split:]]
        orders = [bits, bits[::-1]]
        kept = []
        for hop in range(len(bits)):
            gots = [
                lax.ppermute(part, "feat", [(d, d ^ order[hop]) for d in range(feat)])
                for part, order in zip(parts, orders)
            ]
            gots, held = lax.optimization_barrier((gots, beside[hop : hop + 1]))
            kept += [x for x in held if x is not None]
            parts = [part + got for part, got in zip(parts, gots)]
        return jnp.concatenate(parts, axis=0), kept

    def other_core_across(x):
        pairs = [
            (s * feat + f, (s ^ 1) * feat + (f ^ 1)) for s in range(samp) for f in range(feat)
        ]
        return lax.ppermute(x, ("samp", "feat"), pairs)

    sent = first_pass(start_block, differences, 1 - core)
    got = [other_core(piece) for piece in sent[2:]]
    own_half = first_pass(start_block, differences, core, sent[0])
    pull = first_chunk(meta, differences, got[0])
    summed, (pull,) = over_feat(own_half[0], [None, pull])
    mine = summed.astype(BF16)
    theirs = other_core_across(mine)

    for step in range(ITERS):
        last = step == ITERS - 1
        proj = jnp.concatenate([mine, theirs], axis=1)
        quads, gram, totals, pull = pulled_steps(
            meta, proj, pull, differences, got, (swap, inner), WIDTH, last
        )
        if not last:
            quad = quads[0]
            both = jnp.concatenate([quad[:, :rows], gram], axis=1)
            far = jnp.concatenate([quad[:, rows:], gram], axis=1)
            both, _ = over_feat(both + other_core(far))
            mine = next_projection(both[:, rows:], both[:, :rows])
            theirs = other_core(mine)

    totals_far = [other_core(total) for total in totals]
    scores = score_parts(gram, quads, own_half[1], sent[1], samp // 2)
    hops = [("samp", samp, 1)] + [("feat", feat, bit) for bit in bits]
    score_hops = [2, 4, 1]
    for (axis, size, bit), score_bit in zip(hops, score_hops):
        gram_got = lax.ppermute(gram, axis, [(d, d ^ bit) for d in range(size)])
        scores_got = lax.ppermute(scores, "samp", [(d, d ^ score_bit) for d in range(samp)])
        gram_got, scores_got, totals_far = lax.optimization_barrier(
            (gram_got, scores_got, totals_far)
        )
        gram = gram + gram_got
        if score_bit != 1:
            scores = scores + scores_got
    inverse, layer_scores = scores_of(meta, gram, scores, scores_got, layers_half, features)
    directions = make_directions(meta, inverse, totals, totals_far, math.sqrt(features))
    return (directions, layer_scores)


def orthonormal(pulled, gram):
    lower = jnp.linalg.cholesky(gram)
    return lax.linalg.triangular_solve(lower, pulled, left_side=True, lower=True)


def plain(samp, feat, differences, start_block):
    features = differences.shape[1] * feat
    block = start_block
    basis = None
    for step in range(ITERS):
        partial_rows = dot_nt(block, differences)
        projected = lax.psum(partial_rows, "feat").astype(BF16)
        partial_cols = jnp.dot(projected, differences, preferred_element_type=F32)
        pulled = lax.psum(partial_cols, "samp")
        local_gram = jnp.dot(pulled, pulled.T, precision=HIGHEST)
        gram = lax.psum(local_gram, "feat")
        basis = orthonormal(pulled, gram)
        block = basis.astype(BF16)
    directions = basis * math.sqrt(features)
    samples = differences.shape[0]
    layers_here = differences.shape[1] // WIDTH
    stacked = differences.reshape(samples, layers_here, WIDTH)
    block_layers = block.reshape(block.shape[0], layers_here, WIDTH)
    along = jnp.einsum("kjw,sjw->jks", block_layers, stacked, preferred_element_type=F32)
    captured = jnp.sum(along * along, axis=2)
    energy = jnp.einsum("sjw,sjw->j", stacked, stacked, preferred_element_type=F32)
    captured, energy = lax.psum((captured, energy), "samp")
    layer_scores = features * captured / (energy[:, None] + 1e-06)
    return (directions, layer_scores)


def solution(mesh):
    samp, feat = mesh.shape["samp"], mesh.shape["feat"]

    def on_device(differences, start_block):
        even = differences.shape[1] % (2 * WIDTH) == 0 and differences.shape[0] % 16 == 0
        paired = samp == 8 and feat == 4
        form = pipelined if even and paired else plain
        return form(samp, feat, differences, start_block)

    in_specs = (P("samp", "feat"), P(None, "feat"))
    out_specs = (P(None, "feat"), P("feat", None))
    return jax.shard_map(
        on_device, mesh=mesh, in_specs=in_specs, out_specs=out_specs, check_vma=False
    )
```

```python
import functools
import math

import jax
import jax.numpy as jnp
from jax import lax
from jax.experimental import pallas as pl
from jax.experimental.pallas import tpu as pltpu
from jax.sharding import PartitionSpec as P

WIDTH = 8192
ITERS = 2
F32 = jnp.float32
BF16 = jnp.bfloat16
HIGHEST = lax.Precision.HIGHEST
MIB = 1024 * 1024
PASS_LIMIT = 16 * MIB
STEP_LIMIT = 19 * MIB
SMALL_LIMIT = 4 * MIB
LAST_LIMIT = 20 * MIB

TILE = 1024
SLOTS = 6
PLAN = (1,) * 8
JOINS = 4
PIECES = (1, 1, 2)

VMEM = pl.BlockSpec(memory_space=pltpu.VMEM)
SMEM = pl.BlockSpec(memory_space=pltpu.SMEM)
ANY = pl.BlockSpec(memory_space=pl.ANY)
BLOCK = 512


def dot_nt(a, b):
    return lax.dot_general(a, b, (((1,), (1,)), ((), ())), preferred_element_type=F32)


def dot_nn(a, b, precision=None):
    return lax.dot_general(
        a, b, (((1,), (0,)), ((), ())), precision=precision, preferred_element_type=F32
    )


def spans(half, plan):
    unit = half // sum(plan)
    return [(sum(plan[:i]) * unit, size * unit) for i, size in enumerate(plan)]


def part_of(plan, half, column):
    return [first <= column < first + width for first, width in spans(half, plan)].index(True)


def first_pass_kernel(send, steps, per_layer, side_ref, block_ref, diff_ref, *refs):
    begun = None if send else refs[0]
    refs = refs if send else refs[1:]
    proj_ref, energy_ref = refs[0], refs[1]
    tiles, blocks, in_sems, block_sems, out_sems = refs[-5:]
    base = side_ref[0] * (steps * TILE)

    def columns(i):
        return pl.ds(pl.multiple_of(base + i * TILE, TILE), TILE)

    loads, stores = [], []
    for i in range(steps):
        at = i % SLOTS
        loads.append(
            (
                pltpu.make_async_copy(diff_ref.at[:, columns(i)], tiles.at[at], in_sems.at[at]),
                pltpu.make_async_copy(block_ref.at[:, columns(i)], blocks.at[at], block_sems.at[at]),
            )
        )
        if send:
            piece = part_of(PIECES, steps * TILE, i * TILE)
            inside = i * TILE - spans(steps * TILE, PIECES)[piece][0]
            place = refs[2 + piece].at[:, pl.ds(inside, TILE)]
            stores.append(pltpu.make_async_copy(tiles.at[at], place, out_sems.at[at]))
    ahead = SLOTS - 1
    for load in loads[:ahead]:
        load[0].start()
        load[1].start()
    proj = None
    for i in range(steps):
        at = i % SLOTS
        loads[i][0].wait()
        loads[i][1].wait()
        if send:
            stores[i].start()
        if i + ahead < steps:
            if send and i:
                stores[i - 1].wait()
            loads[i + ahead][0].start()
            loads[i + ahead][1].start()
        part = dot_nt(blocks[at], tiles[at])
        proj = part if proj is None else proj + part
        acc = jnp.zeros((8, TILE), F32)
        for r in range(0, tiles.shape[1], 16):
            rows = tiles[at, r : r + 16, :].astype(F32)
            acc = acc + rows[:8] * rows[:8] + rows[8:] * rows[8:]
        folded = acc[:, :128]
        for j in range(1, TILE // 128):
            folded = folded + acc[:, j * 128 : (j + 1) * 128]
        layer = pl.ds(i // per_layer * 8, 8)
        if i % per_layer:
            folded = folded + energy_ref[layer, :]
        energy_ref[layer, :] = folded
    proj_ref[...] = proj if begun is None else proj + begun[...]
    for store in stores[-SLOTS:]:
        store.wait()


def first_pass(block, differences, side, begun=None):
    send = begun is None
    rows, cols = differences.shape
    k = block.shape[0]
    half = cols // 2
    widths = [width for _, width in spans(half, PIECES)] if send else []
    return pl.pallas_call(
        functools.partial(first_pass_kernel, send, half // TILE, WIDTH // TILE),
        out_shape=[
            jax.ShapeDtypeStruct((k, rows), F32),
            jax.ShapeDtypeStruct((half // WIDTH * 8, 128), F32),
        ]
        + [jax.ShapeDtypeStruct((rows, width), BF16) for width in widths],
        in_specs=[SMEM, ANY, ANY] + [VMEM] * (not send),
        out_specs=[VMEM, VMEM] + [ANY] * len(widths),
        scratch_shapes=[
            pltpu.VMEM((SLOTS, rows, TILE), BF16),
            pltpu.VMEM((SLOTS, k, TILE), BF16),
            pltpu.SemaphoreType.DMA((SLOTS,)),
            pltpu.SemaphoreType.DMA((SLOTS,)),
            pltpu.SemaphoreType.DMA((SLOTS,)),
        ],
        cost_estimate=pl.CostEstimate(
            flops=2 * k * rows * half, bytes_accessed=rows * half * 4, transcendentals=0
        ),
        compiler_params=pltpu.CompilerParams(vmem_limit_bytes=PASS_LIMIT),
        name="first_pass_send" if send else "first_pass",
    )(side.reshape(1).astype(jnp.int32), block, differences, *([] if send else [begun]))


def fetch(core, diff, piece, chunk, out, sems):
    rows, cols = diff.shape
    first, width = chunk
    inside = first - spans(cols // 2, PIECES)[part_of(PIECES, cols // 2, first)][0]
    start = pl.multiple_of(core * (cols // 2) + first, BLOCK)
    mine = diff.at[:, pl.ds(start, width)]
    theirs = piece.at[:, pl.ds(inside, width)]
    return [
        pltpu.make_async_copy(mine, out.at[pl.ds(0, rows), :], sems.at[0]),
        pltpu.make_async_copy(theirs, out.at[pl.ds(rows, rows), :], sems.at[1]),
    ]


def step_kernel(ins, outs, pull_next, quad_next, *refs):
    r = dict(zip(list(ins) + list(outs) + ["pull_sems", "quad_sems"], refs))
    mid = r["meta"][0] > 0
    copies = []
    for name, chunk in (("pull", pull_next), ("quad", quad_next)):
        if chunk is not None:
            place = (r[name + "_piece"], chunk, r[name + "_out"], r[name + "_sems"])
            copies += fetch(r["meta"][1], r["diff"], *place)
    for copy in copies:
        copy.start()
    if "pair" in r:
        for c in range(0, r["pair"].shape[1], BLOCK):
            at = pl.ds(c, BLOCK)
            r["pair"][:, at] = (r["own2"][:, at] + r["got_x"][:, at].astype(F32)).astype(BF16)
    if "send_x" in r:
        pulled = r["own"].shape[1] if "own" in r else 0
        summed = r["pair2"].shape[1] if "pair2" in r else 0
        for c in range(0, max(pulled, summed), BLOCK):
            at = pl.ds(c, BLOCK)
            sent = None
            if c < pulled:
                sent = dot_nn(r["proj"][...], r["pull_in"][:, at])
                r["own"][:, at] = sent
            if c < summed:
                total = r["pair2"][:, at].astype(F32) + r["got_y"][:, at].astype(F32)
                sent = total if sent is None else jnp.where(mid, total, sent)
            r["send_x"][:, at] = sent.astype(BF16)
    if "quad_in" in r:
        width = r["quad_in"].shape[1]
        done = jnp.where(mid, r["sent_x2"][:, :width], r["got_x"][:, :width])
        if "total" in r:
            joined = r["total"].shape[1] - width
            if joined:
                r["total"][:, pl.ds(0, joined)] = r["total_in"][...]
            r["total"][:, pl.ds(joined, width)] = done
        quad = dot_nt(done, r["quad_in"][...])
        gram = dot_nt(done, done)
        r["quad"][...] = quad + r["quad_sum"][...] if "quad_sum" in r else quad
        r["gram"][...] = gram + r["gram_sum"][...] if "gram_sum" in r else gram
    for copy in copies:
        copy.wait()


def first_chunk_kernel(chunk, meta_ref, diff_ref, piece_ref, out_ref, sems):
    copies = fetch(meta_ref[1], diff_ref, piece_ref, chunk, out_ref, sems)
    for copy in copies:
        copy.start()
    for copy in copies:
        copy.wait()


def first_chunk(meta, differences, piece):
    rows, cols = differences.shape
    chunk = spans(cols // 2, PLAN)[0]
    return pl.pallas_call(
        functools.partial(first_chunk_kernel, chunk),
        out_shape=jax.ShapeDtypeStruct((2 * rows, chunk[1]), BF16),
        in_specs=[SMEM, ANY, ANY],
        out_specs=VMEM,
        scratch_shapes=[pltpu.SemaphoreType.DMA((2,))],
        compiler_params=pltpu.CompilerParams(vmem_limit_bytes=STEP_LIMIT),
        name="first_chunk",
    )(meta, differences, piece)


def call_step(name, ins, outs, nexts):
    result = pl.pallas_call(
        functools.partial(step_kernel, tuple(ins), tuple(outs), *nexts),
        out_shape=[jax.ShapeDtypeStruct(*outs[name]) for name in outs],
        in_specs=[spec for _, spec in ins.values()],
        out_specs=[VMEM] * len(outs),
        scratch_shapes=[pltpu.SemaphoreType.DMA((2,)), pltpu.SemaphoreType.DMA((2,))],
        cost_estimate=pl.CostEstimate(flops=2**20, bytes_accessed=2**20, transcendentals=0),
        compiler_params=pltpu.CompilerParams(vmem_limit_bytes=STEP_LIMIT),
        name=name,
    )(*[value for value, _ in ins.values()])
    return dict(zip(outs, result))


def pulled_steps(meta, proj, pull, differences, got, perms, layer, last):
    rows, cols = differences.shape
    k = proj.shape[0]
    half = cols // 2
    chunks = spans(half, PLAN)
    n = len(chunks)
    swap, inner = perms
    group = layer if last else half
    join = half // JOINS
    own, sent, pair, got_x, got_y = {}, {}, {}, {}, {}
    quads, quad, quad_buf, gram = [], None, None, None
    totals, total = [], None
    steps = n + 6
    for t in range(steps):
        front, back = {"meta": (meta, SMEM)}, {"meta": (meta, SMEM)}
        front_outs, back_outs = {}, {}
        chunk = t - 6
        width = 0
        if t < n:
            width = chunks[t][1]
            front["proj"] = (proj, VMEM)
            front["pull_in"] = (pull, VMEM)
            front_outs["own"] = ((k, width), F32)
        if 2 <= t < n + 2:
            front["own2"] = (own[t - 2], VMEM)
            front["got_x"] = (got_x[t - 2], VMEM)
            front_outs["pair"] = ((k, chunks[t - 2][1]), BF16)
        if 4 <= t < n + 4:
            width = max(width, chunks[t - 4][1])
            front["pair2"] = (pair[t - 2], VMEM)
            front["got_y"] = (got_y[t - 2], VMEM)
        if t < n + 4:
            front_outs["send_x"] = ((k, width), BF16)
        if chunk >= 0:
            first, width = chunks[chunk]
            back["got_x"] = (got_x[t - 2], VMEM)
            back["sent_x2"] = (sent[t - 2], VMEM)
            back["quad_in"] = (quad_buf, VMEM)
            if first % group:
                back["quad_sum"] = (quad, VMEM)
            if chunk:
                back["gram_sum"] = (gram, VMEM)
            back_outs["quad"] = ((k, 2 * rows), F32)
            back_outs["gram"] = ((k, k), F32)
            if last:
                if first % join:
                    back["total_in"] = (total, VMEM)
                back_outs["total"] = ((k, first % join + width), BF16)
        nexts = [[None, None], [None, None]]
        if t + 1 < n or (t == steps - 1 and not last):
            following = chunks[t + 1 if t + 1 < n else 0]
            nexts[t >= n][0] = following
            ins, outs = (back, back_outs) if t >= n else (front, front_outs)
            ins["diff"] = (differences, ANY)
            ins["pull_piece"] = (got[part_of(PIECES, half, following[0])], ANY)
            outs["pull_out"] = ((2 * rows, following[1]), BF16)
        if 0 <= chunk + 1 < n:
            following = chunks[chunk + 1]
            nexts[chunk >= 0][1] = following
            ins, outs = (back, back_outs) if chunk >= 0 else (front, front_outs)
            ins["diff"] = (differences, ANY)
            ins["quad_piece"] = (got[part_of(PIECES, half, following[0])], ANY)
            outs["quad_out"] = ((2 * rows, following[1]), BF16)
        pull, quad_buf = None, None
        if front_outs:
            if gram is not None:
                front["after"] = (gram, VMEM)
            r = call_step(f"pulled_front_{t}", front, front_outs, nexts[0])
            pull, quad_buf = r.get("pull_out"), r.get("quad_out")
            if t < n:
                own[t] = r["own"]
            if 2 <= t < n + 2:
                pair[t] = r["pair"]
                got_y[t] = lax.ppermute(pair[t], "samp", inner)
            sent[t] = r["send_x"]
            got_x[t] = lax.ppermute(sent[t], "samp", swap)
            back["after"] = (sent[t], VMEM)
        if back_outs:
            r = call_step(f"pulled_back_{t}", back, back_outs, nexts[1])
            pull, quad_buf = r.get("pull_out", pull), r.get("quad_out")
            quad, gram, total = r["quad"], r["gram"], r.get("total")
            if (first + width) % group == 0:
                quads.append(quad)
            if last and (first + width) % join == 0:
                totals.append(total)
    return quads, gram, totals, pull


def inverse_factor(gram):
    k = gram.shape[0]
    lane = lax.broadcasted_iota(jnp.int32, (8, 2 * k), 1)
    sub = lax.broadcasted_iota(jnp.int32, (8, 2 * k), 0)
    blocks = []
    for b in range(k // 8):
        left = jnp.concatenate([gram[b * 8 : (b + 1) * 8, :], jnp.zeros((8, k), F32)], axis=1)
        blocks.append(jnp.where(lane == sub + (k + b * 8), 1.0, left))
    scale = [jnp.zeros((8, 1), F32) for _ in blocks]
    sub1 = lax.broadcasted_iota(jnp.int32, (8, 1), 0)
    for j in range(k):
        b, i = divmod(j, 8)
        row = blocks[b][i : i + 1, :]
        pivot = row[:, j : j + 1]
        scale[b] = jnp.where(sub1 == i, pivot, scale[b])
        scaled = row / pivot
        for c in range(b, k // 8):
            factor = blocks[c][:, j : j + 1]
            if c == b:
                factor = jnp.where(sub1 > i, factor, 0.0)
            blocks[c] = blocks[c] - factor * scaled
    return jnp.concatenate(
        [block[:, k:] * (1.0 / jnp.sqrt(s)) for block, s in zip(blocks, scale)], axis=0
    )


def project_kernel(gram_ref, quad_ref, proj_ref):
    inverse = inverse_factor(gram_ref[...])
    proj_ref[...] = dot_nn(inverse, quad_ref[...], HIGHEST).astype(BF16)


def next_projection(gram, quad):
    return pl.pallas_call(
        project_kernel,
        out_shape=jax.ShapeDtypeStruct(quad.shape, BF16),
        in_specs=[VMEM, VMEM],
        out_specs=VMEM,
        compiler_params=pltpu.CompilerParams(vmem_limit_bytes=SMALL_LIMIT),
        name="next_projection",
    )(gram, quad)


def score_parts_kernel(groups, chips, gram_ref, kept_ref, sent_ref, *refs):
    quads, out_ref = refs[:groups], refs[groups]
    k = gram_ref.shape[0]
    row = lax.broadcasted_iota(jnp.int32, (k, k), 0)
    lane = lax.broadcasted_iota(jnp.int32, (k, k), 1)
    trace = jnp.sum(jnp.where(row == lane, gram_ref[...], 0.0), keepdims=True)
    scale = 1.0 / jnp.sqrt(trace)
    sub = lax.broadcasted_iota(jnp.int32, (8, k), 0)
    for g in range(groups):
        quad = quads[g][...] * scale
        at = pl.ds(g * k, k)
        out_ref[pl.ds(0, k), at] = lax.dot_general(
            quad,
            quad,
            (((1,), (1,)), ((), ())),
            precision=HIGHEST,
            preferred_element_type=F32,
        )
        kept = jnp.sum(kept_ref[pl.ds(g * 8, 8), :], keepdims=True)
        sent = jnp.sum(sent_ref[pl.ds(g * 8, 8), :], keepdims=True)
        rest = jnp.where(sub == 0, kept, jnp.where(sub == 1, sent, trace / chips))
        out_ref[pl.ds(k, 8), at] = rest


def score_parts(gram, quads, kept, sent, chips):
    k = gram.shape[0]
    return pl.pallas_call(
        functools.partial(score_parts_kernel, len(quads), chips),
        out_shape=jax.ShapeDtypeStruct((k + 8, len(quads) * k), F32),
        in_specs=[VMEM] * (3 + len(quads)),
        out_specs=VMEM,
        compiler_params=pltpu.CompilerParams(vmem_limit_bytes=SMALL_LIMIT),
        name="score_parts",
    )(gram, kept, sent, *quads)


def scores_kernel(groups, features, meta_ref, gram_ref, mine_ref, got_ref, inverse_ref, out_ref):
    k = gram_ref.shape[0]
    inverse = inverse_factor(gram_ref[...])
    inverse_ref[...] = inverse
    core = meta_ref[1]
    ones = jnp.ones((8, k), F32)
    mine, got = mine_ref[...], got_ref[...]
    low, high = jnp.where(core == 0, mine, got), jnp.where(core == 0, got, mine)
    for half, (one, two) in enumerate(((low, high), (high, low))):
        scaled = inverse * jnp.sqrt(one[k + 2 : k + 3, 0:1])
        for g in range(groups):
            at = slice(g * k, (g + 1) * k)
            moment = dot_nn(scaled, one[:k, at], HIGHEST) * scaled
            captured = lax.dot_general(
                ones,
                moment,
                (((1,), (1,)), ((), ())),
                precision=HIGHEST,
                preferred_element_type=F32,
            )[:1]
            energy = one[k : k + 1, at] + two[k + 1 : k + 2, at]
            out_ref[pl.ds(half * groups + g, 1), :] = features * captured / (energy + 1e-06)


def scores_of(meta, gram, mine, got, groups, features):
    k = gram.shape[0]
    return pl.pallas_call(
        functools.partial(scores_kernel, groups, features),
        out_shape=[
            jax.ShapeDtypeStruct((k, k), F32),
            jax.ShapeDtypeStruct((2 * groups, k), F32),
        ],
        in_specs=[SMEM, VMEM, VMEM, VMEM],
        out_specs=[VMEM, VMEM],
        compiler_params=pltpu.CompilerParams(vmem_limit_bytes=SMALL_LIMIT),
        name="scores",
    )(meta, gram, mine, got)


def directions_kernel(count, scale, meta_ref, inverse_ref, *refs):
    totals = refs[: 2 * count]
    out_ref, in_buf, out_buf, in_sems, out_sems = refs[2 * count :]
    core = meta_ref[1]
    width = totals[0].shape[1]
    loads = [
        pltpu.make_async_copy(totals[i], in_buf.at[i], in_sems.at[i]) for i in range(2 * count)
    ]
    for load in loads:
        load.start()
    inverse = inverse_ref[...] * scale
    high = inverse.astype(BF16)
    low = (inverse - high.astype(F32)).astype(BF16)
    stores = []
    for i in range(2 * count):
        loads[i].wait()
        for c in range(0, width, BLOCK):
            at = pl.ds(c, BLOCK)
            piece = in_buf[i, :, at]
            out_buf[i, :, at] = dot_nn(high, piece) + dot_nn(low, piece)
        side = core if i < count else 1 - core
        start = pl.multiple_of((side * count + i % count) * width, width)
        store = pltpu.make_async_copy(
            out_buf.at[i], out_ref.at[:, pl.ds(start, width)], out_sems.at[i]
        )
        store.start()
        stores.append(store)
    for store in stores:
        store.wait()


def make_directions(meta, inverse, totals, totals_far, scale):
    count = len(totals)
    k, width = totals[0].shape
    return pl.pallas_call(
        functools.partial(directions_kernel, count, scale),
        out_shape=jax.ShapeDtypeStruct((k, 2 * count * width), F32),
        in_specs=[SMEM, VMEM] + [ANY] * (2 * count),
        out_specs=ANY,
        scratch_shapes=[
            pltpu.VMEM((2 * count, k, width), BF16),
            pltpu.VMEM((2 * count, k, width), F32),
            pltpu.SemaphoreType.DMA((2 * count,)),
            pltpu.SemaphoreType.DMA((2 * count,)),
        ],
        cost_estimate=pl.CostEstimate(
            flops=8 * k * k * count * width,
            bytes_accessed=12 * k * count * width,
            transcendentals=0,
        ),
        compiler_params=pltpu.CompilerParams(vmem_limit_bytes=LAST_LIMIT),
        name="directions",
    )(meta, inverse, *totals, *totals_far)


def pipelined(samp, feat, differences, start_block):
    rows, cols = differences.shape
    layers_half = cols // WIDTH // 2
    features = cols * feat
    me = lax.axis_index("samp")
    core = me % 2
    chip = me // 2
    mid = (chip == 1) | (chip == 2)
    meta = jnp.stack([mid.astype(jnp.int32), core.astype(jnp.int32)])

    cores = [(d, d ^ 1) for d in range(samp)]
    swap = [(d, d ^ 2) for d in range(samp)]
    inner = [(d, d ^ 6 if d // 2 in (1, 2) else d ^ 1) for d in range(samp)]
    bits = [1 << b for b in range(feat.bit_length() - 1)]

    def other_core(x):
        return lax.ppermute(x, "samp", cores)

    def over_feat(x):
        split = x.shape[0] // 2
        parts = [x[:split], x[split:]]
        orders = [bits, bits[::-1]]
        for hop in range(len(bits)):
            gots = [
                lax.ppermute(part, "feat", [(d, d ^ order[hop]) for d in range(feat)])
                for part, order in zip(parts, orders)
            ]
            gots = lax.optimization_barrier(gots)
            parts = [part + got for part, got in zip(parts, gots)]
        return jnp.concatenate(parts, axis=0)

    def other_core_across(x):
        pairs = [
            (s * feat + f, (s ^ 1) * feat + (f ^ 1)) for s in range(samp) for f in range(feat)
        ]
        return lax.ppermute(x, ("samp", "feat"), pairs)

    sent = first_pass(start_block, differences, 1 - core)
    got = [other_core(piece) for piece in sent[2:]]
    own_half = first_pass(start_block, differences, core, sent[0])
    pull = first_chunk(meta, differences, got[0])
    summed = over_feat(own_half[0])
    mine = summed.astype(BF16)
    theirs, pull = lax.optimization_barrier((other_core_across(mine), pull))

    for step in range(ITERS):
        last = step == ITERS - 1
        proj = jnp.concatenate([mine, theirs], axis=1)
        quads, gram, totals, pull = pulled_steps(
            meta, proj, pull, differences, got, (swap, inner), WIDTH, last
        )
        if not last:
            quad = quads[0]
            both = jnp.concatenate([quad[:, :rows], gram], axis=1)
            far = jnp.concatenate([quad[:, rows:], gram], axis=1)
            both = over_feat(both + other_core(far))
            mine = next_projection(both[:, rows:], both[:, :rows])
            theirs = other_core(mine)

    totals_far = [other_core(total) for total in totals]
    scores = score_parts(gram, quads, own_half[1], sent[1], samp // 2)
    hops = [("samp", samp, 1)] + [("feat", feat, bit) for bit in bits]
    score_hops = [2, 4, 1]
    for (axis, size, bit), score_bit in zip(hops, score_hops):
        gram_got = lax.ppermute(gram, axis, [(d, d ^ bit) for d in range(size)])
        scores_got = lax.ppermute(scores, "samp", [(d, d ^ score_bit) for d in range(samp)])
        gram_got, scores_got, totals_far = lax.optimization_barrier(
            (gram_got, scores_got, totals_far)
        )
        gram = gram + gram_got
        if score_bit != 1:
            scores = scores + scores_got
    inverse, layer_scores = scores_of(meta, gram, scores, scores_got, layers_half, features)
    directions = make_directions(meta, inverse, totals, totals_far, math.sqrt(features))
    return (directions, layer_scores)


def orthonormal(pulled, gram):
    lower = jnp.linalg.cholesky(gram)
    return lax.linalg.triangular_solve(lower, pulled, left_side=True, lower=True)


def plain(samp, feat, differences, start_block):
    features = differences.shape[1] * feat
    block = start_block
    basis = None
    for step in range(ITERS):
        partial_rows = dot_nt(block, differences)
        projected = lax.psum(partial_rows, "feat").astype(BF16)
        partial_cols = jnp.dot(projected, differences, preferred_element_type=F32)
        pulled = lax.psum(partial_cols, "samp")
        local_gram = jnp.dot(pulled, pulled.T, precision=HIGHEST)
        gram = lax.psum(local_gram, "feat")
        basis = orthonormal(pulled, gram)
        block = basis.astype(BF16)
    directions = basis * math.sqrt(features)
    samples = differences.shape[0]
    layers_here = differences.shape[1] // WIDTH
    stacked = differences.reshape(samples, layers_here, WIDTH)
    block_layers = block.reshape(block.shape[0], layers_here, WIDTH)
    along = jnp.einsum("kjw,sjw->jks", block_layers, stacked, preferred_element_type=F32)
    captured = jnp.sum(along * along, axis=2)
    energy = jnp.einsum("sjw,sjw->j", stacked, stacked, preferred_element_type=F32)
    captured, energy = lax.psum((captured, energy), "samp")
    layer_scores = features * captured / (energy[:, None] + 1e-06)
    return (directions, layer_scores)


def solution(mesh):
    samp, feat = mesh.shape["samp"], mesh.shape["feat"]

    def on_device(differences, start_block):
        even = differences.shape[1] % (2 * WIDTH) == 0 and differences.shape[0] % 16 == 0
        paired = samp == 8 and feat == 4
        form = pipelined if even and paired else plain
        return form(samp, feat, differences, start_block)

    in_specs = (P("samp", "feat"), P(None, "feat"))
    out_specs = (P(None, "feat"), P("feat", None))
    return jax.shard_map(
        on_device, mesh=mesh, in_specs=in_specs, out_specs=out_specs, check_vma=False
    )
```

```python
import functools
import math

import jax
import jax.numpy as jnp
from jax import lax
from jax.experimental import pallas as pl
from jax.experimental.pallas import tpu as pltpu
from jax.sharding import PartitionSpec as P

WIDTH = 8192
ITERS = 2
F32 = jnp.float32
BF16 = jnp.bfloat16
HIGHEST = lax.Precision.HIGHEST
MIB = 1024 * 1024
PASS_LIMIT = 16 * MIB
STEP_LIMIT = 16 * MIB
SMALL_LIMIT = 4 * MIB
LAST_LIMIT = 20 * MIB

TILE = 1024
SLOTS = 6
PLAN = (1,) * 8
JOINS = 4
PIECES = (1, 1, 2)

VMEM = pl.BlockSpec(memory_space=pltpu.VMEM)
SMEM = pl.BlockSpec(memory_space=pltpu.SMEM)
ANY = pl.BlockSpec(memory_space=pl.ANY)
BLOCK = 512


def dot_nt(a, b):
    return lax.dot_general(a, b, (((1,), (1,)), ((), ())), preferred_element_type=F32)


def dot_nn(a, b, precision=None):
    return lax.dot_general(
        a, b, (((1,), (0,)), ((), ())), precision=precision, preferred_element_type=F32
    )


def spans(half, plan):
    unit = half // sum(plan)
    return [(sum(plan[:i]) * unit, size * unit) for i, size in enumerate(plan)]


def part_of(plan, half, column):
    return [first <= column < first + width for first, width in spans(half, plan)].index(True)


def first_pass_kernel(send, steps, per_layer, side_ref, block_ref, diff_ref, *refs):
    begun = None if send else refs[0]
    refs = refs if send else refs[1:]
    proj_ref, energy_ref = refs[0], refs[1]
    tiles, blocks, in_sems, block_sems, out_sems = refs[-5:]
    base = side_ref[0] * (steps * TILE)

    def columns(i):
        return pl.ds(pl.multiple_of(base + i * TILE, TILE), TILE)

    loads, stores = [], []
    for i in range(steps):
        at = i % SLOTS
        loads.append(
            (
                pltpu.make_async_copy(diff_ref.at[:, columns(i)], tiles.at[at], in_sems.at[at]),
                pltpu.make_async_copy(block_ref.at[:, columns(i)], blocks.at[at], block_sems.at[at]),
            )
        )
        if send:
            piece = part_of(PIECES, steps * TILE, i * TILE)
            inside = i * TILE - spans(steps * TILE, PIECES)[piece][0]
            place = refs[2 + piece].at[:, pl.ds(inside, TILE)]
            stores.append(pltpu.make_async_copy(tiles.at[at], place, out_sems.at[at]))
    ahead = SLOTS - 1
    for load in loads[:ahead]:
        load[0].start()
        load[1].start()
    proj = None
    for i in range(steps):
        at = i % SLOTS
        loads[i][0].wait()
        loads[i][1].wait()
        if send:
            stores[i].start()
        if i + ahead < steps:
            if send and i:
                stores[i - 1].wait()
            loads[i + ahead][0].start()
            loads[i + ahead][1].start()
        part = dot_nt(blocks[at], tiles[at])
        proj = part if proj is None else proj + part
        acc = jnp.zeros((8, TILE), F32)
        for r in range(0, tiles.shape[1], 16):
            rows = tiles[at, r : r + 16, :].astype(F32)
            acc = acc + rows[:8] * rows[:8] + rows[8:] * rows[8:]
        folded = acc[:, :128]
        for j in range(1, TILE // 128):
            folded = folded + acc[:, j * 128 : (j + 1) * 128]
        layer = pl.ds(i // per_layer * 8, 8)
        if i % per_layer:
            folded = folded + energy_ref[layer, :]
        energy_ref[layer, :] = folded
    proj_ref[...] = proj if begun is None else proj + begun[...]
    for store in stores[-SLOTS:]:
        store.wait()


def first_pass(block, differences, side, begun=None):
    send = begun is None
    rows, cols = differences.shape
    k = block.shape[0]
    half = cols // 2
    widths = [width for _, width in spans(half, PIECES)] if send else []
    return pl.pallas_call(
        functools.partial(first_pass_kernel, send, half // TILE, WIDTH // TILE),
        out_shape=[
            jax.ShapeDtypeStruct((k, rows), F32),
            jax.ShapeDtypeStruct((half // WIDTH * 8, 128), F32),
        ]
        + [jax.ShapeDtypeStruct((rows, width), BF16) for width in widths],
        in_specs=[SMEM, ANY, ANY] + [VMEM] * (not send),
        out_specs=[VMEM, VMEM] + [ANY] * len(widths),
        scratch_shapes=[
            pltpu.VMEM((SLOTS, rows, TILE), BF16),
            pltpu.VMEM((SLOTS, k, TILE), BF16),
            pltpu.SemaphoreType.DMA((SLOTS,)),
            pltpu.SemaphoreType.DMA((SLOTS,)),
            pltpu.SemaphoreType.DMA((SLOTS,)),
        ],
        cost_estimate=pl.CostEstimate(
            flops=2 * k * rows * half, bytes_accessed=rows * half * 4, transcendentals=0
        ),
        compiler_params=pltpu.CompilerParams(vmem_limit_bytes=PASS_LIMIT),
        name="first_pass_send" if send else "first_pass",
    )(side.reshape(1).astype(jnp.int32), block, differences, *([] if send else [begun]))


def fetch(core, diff, piece, chunk, out, sems):
    rows, cols = diff.shape
    first, width = chunk
    inside = first - spans(cols // 2, PIECES)[part_of(PIECES, cols // 2, first)][0]
    start = pl.multiple_of(core * (cols // 2) + first, BLOCK)
    mine = diff.at[:, pl.ds(start, width)]
    theirs = piece.at[:, pl.ds(inside, width)]
    return [
        pltpu.make_async_copy(mine, out.at[pl.ds(0, rows), :], sems.at[0]),
        pltpu.make_async_copy(theirs, out.at[pl.ds(rows, rows), :], sems.at[1]),
    ]


def step_kernel(ins, outs, pull_next, quad_next, *refs):
    r = dict(zip(list(ins) + list(outs) + ["pull_sems", "quad_sems"], refs))
    mid = r["meta"][0] > 0
    copies = []
    for name, chunk in (("pull", pull_next), ("quad", quad_next)):
        if chunk is not None:
            place = (r[name + "_piece"], chunk, r[name + "_out"], r[name + "_sems"])
            copies += fetch(r["meta"][1], r["diff"], *place)
    for copy in copies:
        copy.start()
    if "pair" in r:
        for c in range(0, r["pair"].shape[1], BLOCK):
            at = pl.ds(c, BLOCK)
            r["pair"][:, at] = (r["own2"][:, at] + r["got_x"][:, at].astype(F32)).astype(BF16)
    if "send_x" in r:
        pulled = r["own"].shape[1] if "own" in r else 0
        summed = r["pair2"].shape[1] if "pair2" in r else 0
        for c in range(0, max(pulled, summed), BLOCK):
            at = pl.ds(c, BLOCK)
            sent = None
            if c < pulled:
                sent = dot_nn(r["proj"][...], r["pull_in"][:, at])
                r["own"][:, at] = sent
            if c < summed:
                total = r["pair2"][:, at].astype(F32) + r["got_y"][:, at].astype(F32)
                sent = total if sent is None else jnp.where(mid, total, sent)
            r["send_x"][:, at] = sent.astype(BF16)
    if "quad_in" in r:
        width = r["quad_in"].shape[1]
        done = jnp.where(mid, r["sent_x2"][:, :width], r["got_x"][:, :width])
        if "total" in r:
            joined = r["total"].shape[1] - width
            if joined:
                r["total"][:, pl.ds(0, joined)] = r["total_in"][...]
            r["total"][:, pl.ds(joined, width)] = done
        quad = dot_nt(done, r["quad_in"][...])
        gram = dot_nt(done, done)
        r["quad"][...] = quad + r["quad_sum"][...] if "quad_sum" in r else quad
        r["gram"][...] = gram + r["gram_sum"][...] if "gram_sum" in r else gram
    for copy in copies:
        copy.wait()


def first_chunk_kernel(chunk, meta_ref, diff_ref, piece_ref, out_ref, sems):
    copies = fetch(meta_ref[1], diff_ref, piece_ref, chunk, out_ref, sems)
    for copy in copies:
        copy.start()
    for copy in copies:
        copy.wait()


def first_chunk(meta, differences, piece):
    rows, cols = differences.shape
    chunk = spans(cols // 2, PLAN)[0]
    return pl.pallas_call(
        functools.partial(first_chunk_kernel, chunk),
        out_shape=jax.ShapeDtypeStruct((2 * rows, chunk[1]), BF16),
        in_specs=[SMEM, ANY, ANY],
        out_specs=VMEM,
        scratch_shapes=[pltpu.SemaphoreType.DMA((2,))],
        compiler_params=pltpu.CompilerParams(vmem_limit_bytes=STEP_LIMIT),
        name="first_chunk",
    )(meta, differences, piece)


def call_step(name, ins, outs, nexts):
    result = pl.pallas_call(
        functools.partial(step_kernel, tuple(ins), tuple(outs), *nexts),
        out_shape=[jax.ShapeDtypeStruct(*outs[name]) for name in outs],
        in_specs=[spec for _, spec in ins.values()],
        out_specs=[VMEM] * len(outs),
        scratch_shapes=[pltpu.SemaphoreType.DMA((2,)), pltpu.SemaphoreType.DMA((2,))],
        cost_estimate=pl.CostEstimate(flops=2**20, bytes_accessed=2**20, transcendentals=0),
        compiler_params=pltpu.CompilerParams(vmem_limit_bytes=STEP_LIMIT),
        name=name,
    )(*[value for value, _ in ins.values()])
    return dict(zip(outs, result))


def pulled_steps(meta, proj, pull, differences, got, perms, layer, last):
    rows, cols = differences.shape
    k = proj.shape[0]
    half = cols // 2
    chunks = spans(half, PLAN)
    n = len(chunks)
    swap, inner = perms
    group = layer if last else half
    join = half // JOINS
    own, sent, pair, got_x, got_y = {}, {}, {}, {}, {}
    quads, quad, quad_buf, gram = [], None, None, None
    totals, total = [], None
    steps = n + 6
    for t in range(steps):
        front, back = {"meta": (meta, SMEM)}, {"meta": (meta, SMEM)}
        front_outs, back_outs = {}, {}
        chunk = t - 6
        width = 0
        if t < n:
            width = chunks[t][1]
            front["proj"] = (proj, VMEM)
            front["pull_in"] = (pull, VMEM)
            front_outs["own"] = ((k, width), F32)
        if 2 <= t < n + 2:
            front["own2"] = (own[t - 2], VMEM)
            front["got_x"] = (got_x[t - 2], VMEM)
            front_outs["pair"] = ((k, chunks[t - 2][1]), BF16)
        if 4 <= t < n + 4:
            width = max(width, chunks[t - 4][1])
            front["pair2"] = (pair[t - 2], VMEM)
            front["got_y"] = (got_y[t - 2], VMEM)
        if t < n + 4:
            front_outs["send_x"] = ((k, width), BF16)
        if chunk >= 0:
            first, width = chunks[chunk]
            back["got_x"] = (got_x[t - 2], VMEM)
            back["sent_x2"] = (sent[t - 2], VMEM)
            back["quad_in"] = (quad_buf, VMEM)
            if first % group:
                back["quad_sum"] = (quad, VMEM)
            if chunk:
                back["gram_sum"] = (gram, VMEM)
            back_outs["quad"] = ((k, 2 * rows), F32)
            back_outs["gram"] = ((k, k), F32)
            if last:
                if first % join:
                    back["total_in"] = (total, VMEM)
                back_outs["total"] = ((k, first % join + width), BF16)
        nexts = [[None, None], [None, None]]
        if t + 1 < n or (t == steps - 1 and not last):
            following = chunks[t + 1 if t + 1 < n else 0]
            nexts[t >= n][0] = following
            ins, outs = (back, back_outs) if t >= n else (front, front_outs)
            ins["diff"] = (differences, ANY)
            ins["pull_piece"] = (got[part_of(PIECES, half, following[0])], ANY)
            outs["pull_out"] = ((2 * rows, following[1]), BF16)
        if 0 <= chunk + 1 < n:
            following = chunks[chunk + 1]
            nexts[chunk >= 0][1] = following
            ins, outs = (back, back_outs) if chunk >= 0 else (front, front_outs)
            ins["diff"] = (differences, ANY)
            ins["quad_piece"] = (got[part_of(PIECES, half, following[0])], ANY)
            outs["quad_out"] = ((2 * rows, following[1]), BF16)
        pull, quad_buf = None, None
        if front_outs:
            if gram is not None:
                front["after"] = (gram, VMEM)
            r = call_step(f"pulled_front_{t}", front, front_outs, nexts[0])
            pull, quad_buf = r.get("pull_out"), r.get("quad_out")
            if t < n:
                own[t] = r["own"]
            if 2 <= t < n + 2:
                pair[t] = r["pair"]
                got_y[t] = lax.ppermute(pair[t], "samp", inner)
            sent[t] = r["send_x"]
            got_x[t] = lax.ppermute(sent[t], "samp", swap)
            back["after"] = (sent[t], VMEM)
        if back_outs:
            r = call_step(f"pulled_back_{t}", back, back_outs, nexts[1])
            pull, quad_buf = r.get("pull_out", pull), r.get("quad_out")
            quad, gram, total = r["quad"], r["gram"], r.get("total")
            if (first + width) % group == 0:
                quads.append(quad)
            if last and (first + width) % join == 0:
                totals.append(total)
    return quads, gram, totals, pull


def inverse_factor(gram):
    k = gram.shape[0]
    lane = lax.broadcasted_iota(jnp.int32, (8, 2 * k), 1)
    sub = lax.broadcasted_iota(jnp.int32, (8, 2 * k), 0)
    blocks = []
    for b in range(k // 8):
        left = jnp.concatenate([gram[b * 8 : (b + 1) * 8, :], jnp.zeros((8, k), F32)], axis=1)
        blocks.append(jnp.where(lane == sub + (k + b * 8), 1.0, left))
    scale = [jnp.zeros((8, 1), F32) for _ in blocks]
    sub1 = lax.broadcasted_iota(jnp.int32, (8, 1), 0)
    for j in range(k):
        b, i = divmod(j, 8)
        row = blocks[b][i : i + 1, :]
        pivot = row[:, j : j + 1]
        scale[b] = jnp.where(sub1 == i, pivot, scale[b])
        inverse = 1.0 / pivot
        for c in range(b, k // 8):
            factor = blocks[c][:, j : j + 1] * inverse
            if c == b:
                factor = jnp.where(sub1 > i, factor, 0.0)
            blocks[c] = blocks[c] - factor * row
    return jnp.concatenate(
        [block[:, k:] * (1.0 / jnp.sqrt(s)) for block, s in zip(blocks, scale)], axis=0
    )


def project_kernel(gram_ref, quad_ref, proj_ref):
    inverse = inverse_factor(gram_ref[...])
    proj_ref[...] = dot_nn(inverse, quad_ref[...], HIGHEST).astype(BF16)


def next_projection(gram, quad):
    return pl.pallas_call(
        project_kernel,
        out_shape=jax.ShapeDtypeStruct(quad.shape, BF16),
        in_specs=[VMEM, VMEM],
        out_specs=VMEM,
        compiler_params=pltpu.CompilerParams(vmem_limit_bytes=SMALL_LIMIT),
        name="next_projection",
    )(gram, quad)


def score_parts_kernel(groups, chips, gram_ref, kept_ref, sent_ref, *refs):
    quads, out_ref = refs[:groups], refs[groups]
    k = gram_ref.shape[0]
    row = lax.broadcasted_iota(jnp.int32, (k, k), 0)
    lane = lax.broadcasted_iota(jnp.int32, (k, k), 1)
    trace = jnp.sum(jnp.where(row == lane, gram_ref[...], 0.0), keepdims=True)
    scale = 1.0 / jnp.sqrt(trace)
    sub = lax.broadcasted_iota(jnp.int32, (8, k), 0)
    for g in range(groups):
        quad = quads[g][...] * scale
        at = pl.ds(g * k, k)
        out_ref[pl.ds(0, k), at] = lax.dot_general(
            quad,
            quad,
            (((1,), (1,)), ((), ())),
            precision=HIGHEST,
            preferred_element_type=F32,
        )
        kept = jnp.sum(kept_ref[pl.ds(g * 8, 8), :], keepdims=True)
        sent = jnp.sum(sent_ref[pl.ds(g * 8, 8), :], keepdims=True)
        rest = jnp.where(sub == 0, kept, jnp.where(sub == 1, sent, trace / chips))
        out_ref[pl.ds(k, 8), at] = rest


def score_parts(gram, quads, kept, sent, chips):
    k = gram.shape[0]
    return pl.pallas_call(
        functools.partial(score_parts_kernel, len(quads), chips),
        out_shape=jax.ShapeDtypeStruct((k + 8, len(quads) * k), F32),
        in_specs=[VMEM] * (3 + len(quads)),
        out_specs=VMEM,
        compiler_params=pltpu.CompilerParams(vmem_limit_bytes=SMALL_LIMIT),
        name="score_parts",
    )(gram, kept, sent, *quads)


def scores_kernel(groups, features, meta_ref, gram_ref, mine_ref, got_ref, inverse_ref, out_ref):
    k = gram_ref.shape[0]
    inverse = inverse_factor(gram_ref[...])
    inverse_ref[...] = inverse
    core = meta_ref[1]
    ones = jnp.ones((8, k), F32)
    mine, got = mine_ref[...], got_ref[...]
    low, high = jnp.where(core == 0, mine, got), jnp.where(core == 0, got, mine)
    for half, (one, two) in enumerate(((low, high), (high, low))):
        scaled = inverse * jnp.sqrt(one[k + 2 : k + 3, 0:1])
        for g in range(groups):
            at = slice(g * k, (g + 1) * k)
            moment = dot_nn(scaled, one[:k, at], HIGHEST) * scaled
            captured = lax.dot_general(
                ones,
                moment,
                (((1,), (1,)), ((), ())),
                precision=HIGHEST,
                preferred_element_type=F32,
            )[:1]
            energy = one[k : k + 1, at] + two[k + 1 : k + 2, at]
            out_ref[pl.ds(half * groups + g, 1), :] = features * captured / (energy + 1e-06)


def scores_of(meta, gram, mine, got, groups, features):
    k = gram.shape[0]
    return pl.pallas_call(
        functools.partial(scores_kernel, groups, features),
        out_shape=[
            jax.ShapeDtypeStruct((k, k), F32),
            jax.ShapeDtypeStruct((2 * groups, k), F32),
        ],
        in_specs=[SMEM, VMEM, VMEM, VMEM],
        out_specs=[VMEM, VMEM],
        compiler_params=pltpu.CompilerParams(vmem_limit_bytes=SMALL_LIMIT),
        name="scores",
    )(meta, gram, mine, got)


def directions_kernel(count, scale, meta_ref, inverse_ref, *refs):
    totals = refs[: 2 * count]
    out_ref, in_buf, out_buf, in_sems, out_sems = refs[2 * count :]
    core = meta_ref[1]
    width = totals[0].shape[1]
    loads = [
        pltpu.make_async_copy(totals[i], in_buf.at[i], in_sems.at[i]) for i in range(2 * count)
    ]
    for load in loads:
        load.start()
    inverse = inverse_ref[...] * scale
    high = inverse.astype(BF16)
    low = (inverse - high.astype(F32)).astype(BF16)
    stores = []
    for i in range(2 * count):
        loads[i].wait()
        for c in range(0, width, BLOCK):
            at = pl.ds(c, BLOCK)
            piece = in_buf[i, :, at]
            out_buf[i, :, at] = dot_nn(high, piece) + dot_nn(low, piece)
        side = core if i < count else 1 - core
        start = pl.multiple_of((side * count + i % count) * width, width)
        store = pltpu.make_async_copy(
            out_buf.at[i], out_ref.at[:, pl.ds(start, width)], out_sems.at[i]
        )
        store.start()
        stores.append(store)
    for store in stores:
        store.wait()


def make_directions(meta, inverse, totals, totals_far, scale):
    count = len(totals)
    k, width = totals[0].shape
    return pl.pallas_call(
        functools.partial(directions_kernel, count, scale),
        out_shape=jax.ShapeDtypeStruct((k, 2 * count * width), F32),
        in_specs=[SMEM, VMEM] + [ANY] * (2 * count),
        out_specs=ANY,
        scratch_shapes=[
            pltpu.VMEM((2 * count, k, width), BF16),
            pltpu.VMEM((2 * count, k, width), F32),
            pltpu.SemaphoreType.DMA((2 * count,)),
            pltpu.SemaphoreType.DMA((2 * count,)),
        ],
        cost_estimate=pl.CostEstimate(
            flops=8 * k * k * count * width,
            bytes_accessed=12 * k * count * width,
            transcendentals=0,
        ),
        compiler_params=pltpu.CompilerParams(vmem_limit_bytes=LAST_LIMIT),
        name="directions",
    )(meta, inverse, *totals, *totals_far)


def pipelined(samp, feat, differences, start_block):
    rows, cols = differences.shape
    layers_half = cols // WIDTH // 2
    features = cols * feat
    me = lax.axis_index("samp")
    core = me % 2
    chip = me // 2
    mid = (chip == 1) | (chip == 2)
    meta = jnp.stack([mid.astype(jnp.int32), core.astype(jnp.int32)])

    cores = [(d, d ^ 1) for d in range(samp)]
    swap = [(d, d ^ 2) for d in range(samp)]
    inner = [(d, d ^ 6 if d // 2 in (1, 2) else d ^ 1) for d in range(samp)]
    bits = [1 << b for b in range(feat.bit_length() - 1)]

    def other_core(x):
        return lax.ppermute(x, "samp", cores)

    def over_feat(x):
        split = x.shape[0] // 2
        parts = [x[:split], x[split:]]
        orders = [bits, bits[::-1]]
        for hop in range(len(bits)):
            gots = [
                lax.ppermute(part, "feat", [(d, d ^ order[hop]) for d in range(feat)])
                for part, order in zip(parts, orders)
            ]
            gots = lax.optimization_barrier(gots)
            parts = [part + got for part, got in zip(parts, gots)]
        return jnp.concatenate(parts, axis=0)

    def other_core_across(x):
        pairs = [
            (s * feat + f, (s ^ 1) * feat + (f ^ 1)) for s in range(samp) for f in range(feat)
        ]
        return lax.ppermute(x, ("samp", "feat"), pairs)

    sent = first_pass(start_block, differences, 1 - core)
    got = [other_core(piece) for piece in sent[2:]]
    own_half = first_pass(start_block, differences, core, sent[0])
    pull = first_chunk(meta, differences, got[0])
    summed = over_feat(own_half[0])
    mine = summed.astype(BF16)
    theirs, pull = lax.optimization_barrier((other_core_across(mine), pull))

    for step in range(ITERS):
        last = step == ITERS - 1
        proj = jnp.concatenate([mine, theirs], axis=1)
        quads, gram, totals, pull = pulled_steps(
            meta, proj, pull, differences, got, (swap, inner), WIDTH, last
        )
        if not last:
            quad = quads[0]
            both = jnp.concatenate([quad[:, :rows], gram], axis=1)
            far = jnp.concatenate([quad[:, rows:], gram], axis=1)
            both = over_feat(both + other_core(far))
            mine = next_projection(both[:, rows:], both[:, :rows])
            theirs = other_core(mine)

    totals_far = [other_core(total) for total in totals]
    scores = score_parts(gram, quads, own_half[1], sent[1], samp // 2)
    hops = [("samp", samp, 1)] + [("feat", feat, bit) for bit in bits]
    score_hops = [2, 4, 1]
    for (axis, size, bit), score_bit in zip(hops, score_hops):
        gram_got = lax.ppermute(gram, axis, [(d, d ^ bit) for d in range(size)])
        scores_got = lax.ppermute(scores, "samp", [(d, d ^ score_bit) for d in range(samp)])
        gram_got, scores_got, totals_far = lax.optimization_barrier(
            (gram_got, scores_got, totals_far)
        )
        gram = gram + gram_got
        if score_bit != 1:
            scores = scores + scores_got
    inverse, layer_scores = scores_of(meta, gram, scores, scores_got, layers_half, features)
    directions = make_directions(meta, inverse, totals, totals_far, math.sqrt(features))
    return (directions, layer_scores)


def orthonormal(pulled, gram):
    lower = jnp.linalg.cholesky(gram)
    return lax.linalg.triangular_solve(lower, pulled, left_side=True, lower=True)


def plain(samp, feat, differences, start_block):
    features = differences.shape[1] * feat
    block = start_block
    basis = None
    for step in range(ITERS):
        partial_rows = dot_nt(block, differences)
        projected = lax.psum(partial_rows, "feat").astype(BF16)
        partial_cols = jnp.dot(projected, differences, preferred_element_type=F32)
        pulled = lax.psum(partial_cols, "samp")
        local_gram = jnp.dot(pulled, pulled.T, precision=HIGHEST)
        gram = lax.psum(local_gram, "feat")
        basis = orthonormal(pulled, gram)
        block = basis.astype(BF16)
    directions = basis * math.sqrt(features)
    samples = differences.shape[0]
    layers_here = differences.shape[1] // WIDTH
    stacked = differences.reshape(samples, layers_here, WIDTH)
    block_layers = block.reshape(block.shape[0], layers_here, WIDTH)
    along = jnp.einsum("kjw,sjw->jks", block_layers, stacked, preferred_element_type=F32)
    captured = jnp.sum(along * along, axis=2)
    energy = jnp.einsum("sjw,sjw->j", stacked, stacked, preferred_element_type=F32)
    captured, energy = lax.psum((captured, energy), "samp")
    layer_scores = features * captured / (energy[:, None] + 1e-06)
    return (directions, layer_scores)


def solution(mesh):
    samp, feat = mesh.shape["samp"], mesh.shape["feat"]

    def on_device(differences, start_block):
        even = differences.shape[1] % (2 * WIDTH) == 0 and differences.shape[0] % 16 == 0
        paired = samp == 8 and feat == 4
        form = pipelined if even and paired else plain
        return form(samp, feat, differences, start_block)

    in_specs = (P("samp", "feat"), P(None, "feat"))
    out_specs = (P(None, "feat"), P("feat", None))
    return jax.shard_map(
        on_device, mesh=mesh, in_specs=in_specs, out_specs=out_specs, check_vma=False
    )
```
